256 devices in a mesh: group: 16 (over y, x), member: 16 (over z, core).
Axes of the slice: x: 4, y: 4, z: 8, core: 2. Of those that a mesh axis runs over, the one named last changes fastest.
Arguments:
- tokens: bfloat16 [32768, 1024], P(('group', 'member')), may hold values from -420 to 420
- latents: bfloat16 [1024, 1024], P('member'), may hold values from -420 to 420
- tok_gain: float32 [1024], replicated, may hold values from 0.5 to 1.5
- lat_gain: float32 [1024], replicated, may hold values from 0.5 to 1.5
- mlp_gain: float32 [1024], replicated, may hold values from 0.5 to 1.5
- w_ref_tok: bfloat16 [1024, 1024], replicated, may hold values from -1.15625 to 1.15625
- w_val_tok: bfloat16 [1024, 1024], replicated, may hold values from -0.75 to 0.75
- w_out_tok: bfloat16 [1024, 1024], replicated, may hold values from -0.1875 to 0.1875
- w_ref_lat: bfloat16 [1024, 1024], P('member'), may hold values from -1.15625 to 1.15625
- w_val_lat: bfloat16 [1024, 1024], P('member'), may hold values from -0.75 to 0.75
- w_out_lat: bfloat16 [1024, 1024], P('member'), may hold values from -0.1875 to 0.1875
- w_up: bfloat16 [1024, 2048], P(None, 'member'), may hold values from -0.1875 to 0.1875
- w_down: bfloat16 [2048, 1024], P('member'), may hold values from -0.125 to 0.125
Outputs:
- tokens_out: bfloat16 [32768, 1024], P(('group', 'member'))
- latents_out: bfloat16 [1024, 1024], P('member')
The draws below stay inside these ranges and needn't reach their ends.
All inputs are finite; a program needn't handle non-finite values.
Results may differ from the reference program's by a relative error of at most 0.005.
The reference program's roundings to bfloat16 on the way count: a program that leaves them out, or rounds other values in their place, can miss the bound.
Values may be sent and summed in bfloat16 or wider, within the bound.
A program may use at most 128 MiB of HBM per device.

```python
import jax
import jax.numpy as jnp
from jax import lax

D = 1024
HEADS = 16
HEAD_DIM = 64
LATENTS = 1024
FF = 2048
TOKENS = 32768
N_GROUP = 16
N_MEMBER = 16


def latent_rows(key):
    base_rows = jnp.clip(jax.random.normal(jax.random.fold_in(key, 101), (LATENTS, D), jnp.float32), -4.0, 4.0)
    return base_rows


def draw_latents(key, part):
    lat_rows = latent_rows(key)
    return lat_rows.astype(jnp.bfloat16)


def draw_tokens(key, part):
    tok_rows = jnp.clip(jax.random.normal(jax.random.fold_in(key, 201), (TOKENS, D), jnp.float32), -4.0, 4.0)
    return tok_rows.astype(jnp.bfloat16)


def reference_pair(key):
    first_w = jnp.clip(jax.random.normal(jax.random.fold_in(key, 401), (D, D), jnp.float32), -5.0, 5.0) * D ** (-0.5)
    second_w = jnp.clip(jax.random.normal(jax.random.fold_in(key, 402), (D, D), jnp.float32), -5.0, 5.0) * D ** (-0.5)
    return (first_w * 1.6, second_w * 1.6)


def draw_w_ref_tok(key, part):
    return reference_pair(key)[0].astype(jnp.bfloat16)


def draw_w_ref_lat(key, part):
    return reference_pair(key)[1].astype(jnp.bfloat16)


def block_scale(stream_key, extent, split, smallest, largest):
    factor_of = 1.0
    for dim, blocks in split:
        draws = jax.random.uniform(jax.random.fold_in(jax.random.fold_in(stream_key, 6), dim), (blocks,), jnp.float32, smallest / len(split), largest / len(split))
        factor_of = factor_of * jnp.repeat(jnp.exp(draws), extent[dim] // blocks).reshape((-1,) + (1,) * (len(extent) - 1 - dim))
    return factor_of


def bell_draw(key, extent, width, reach, cuts=(), kind=jnp.bfloat16):
    gain = block_scale(key, extent, cuts, -0.22, 0.18) if cuts else 1.0
    drawn = jax.random.normal(key, extent, jnp.float32) * width * gain
    return jnp.minimum(jnp.maximum(drawn, -reach), reach).astype(kind)


def setup_inputs(seed: int = 0) -> dict:
    seeds = jax.random.split(jax.random.key(seed), 14)
    tokens = draw_tokens(jax.random.fold_in(seeds[13], 71), 0)
    latents = draw_latents(jax.random.fold_in(seeds[13], 71), 0)
    tok_gain = jnp.clip(1.0 + 0.1 * jax.random.normal(seeds[2], (D,), jnp.float32), 0.5, 1.5)
    lat_gain = jnp.clip(1.0 + 0.1 * jax.random.normal(seeds[3], (D,), jnp.float32), 0.5, 1.5)
    mlp_gain = jnp.clip(1.0 + 0.1 * jax.random.normal(seeds[4], (D,), jnp.float32), 0.5, 1.5)
    w_ref_tok = draw_w_ref_tok(jax.random.fold_in(seeds[13], 71), 0)
    w_val_tok = bell_draw(seeds[6], (D, D), (D // 16) ** -0.5, 0.75)
    w_out_tok = bell_draw(seeds[7], (D, D), D ** -0.5, 0.1875)
    w_ref_lat = draw_w_ref_lat(jax.random.fold_in(seeds[13], 71), 0)
    w_val_lat = bell_draw(seeds[9], (D, D), (D // 16) ** -0.5, 0.75, ((0, 16),))
    w_out_lat = bell_draw(seeds[10], (D, D), D ** -0.5, 0.1875, ((0, 16),))
    w_up = bell_draw(seeds[11], (D, FF), D ** -0.5, 0.1875, ((1, 16),))
    w_down = bell_draw(seeds[12], (FF, D), FF ** -0.5, 0.125, ((0, 16),))
    return dict(tokens=tokens, latents=latents, tok_gain=tok_gain, lat_gain=lat_gain, mlp_gain=mlp_gain, w_ref_tok=w_ref_tok, w_val_tok=w_val_tok, w_out_tok=w_out_tok, w_ref_lat=w_ref_lat, w_val_lat=w_val_lat, w_out_lat=w_out_lat, w_up=w_up, w_down=w_down)


NORM_EPS = 1e-06

def normalize(values):
    return values * lax.rsqrt(lax.optimization_barrier(jnp.mean(values * values, axis=-1, keepdims=True)) + NORM_EPS)

def project(left_side, right_side):
    return jnp.dot(left_side, right_side, preferred_element_type=jnp.float32)

def reference(tokens, latents, tok_gain, lat_gain, mlp_gain, w_ref_tok, w_val_tok, w_out_tok, w_ref_lat, w_val_lat, w_out_lat, w_up, w_down):
    score_scaling = HEAD_DIM ** (-0.5)
    lat_norm = (normalize(latents.astype(jnp.float32)) * lat_gain).astype(jnp.bfloat16)
    ref_lat = project(lat_norm, w_ref_lat).astype(jnp.bfloat16)
    val_lat = project(lat_norm, w_val_lat).astype(jnp.bfloat16)
    latent_key_rows = ref_lat.astype(jnp.float32).reshape(LATENTS, HEADS, HEAD_DIM)
    latent_value_rows = val_lat.astype(jnp.float32).reshape(LATENTS, HEADS, HEAD_DIM)
    block_count = N_GROUP * N_MEMBER
    row_count = TOKENS // block_count
    token_blocks = tokens.reshape(block_count, row_count, D)

    def advance(running, token_block):
        peak_now, total_now, summed_result = running
        tok_norm = (normalize(token_block.astype(jnp.float32)) * tok_gain).astype(jnp.bfloat16)
        ref_tok = project(tok_norm, w_ref_tok).astype(jnp.bfloat16)
        val_tok = project(tok_norm, w_val_tok).astype(jnp.bfloat16)
        query_rows = ref_tok.astype(jnp.float32).reshape(row_count, HEADS, HEAD_DIM)
        attention_scores = jnp.einsum('fxc,jxc->xfj', query_rows, latent_key_rows, precision=lax.Precision.HIGHEST) * score_scaling
        row_peak = lax.optimization_barrier(jnp.max(attention_scores, axis=2, keepdims=True))
        exponent = jnp.exp(attention_scores - row_peak)
        token_attention_weights = (exponent / lax.optimization_barrier(jnp.sum(exponent, axis=2, keepdims=True))).astype(jnp.bfloat16)
        token_attention = jnp.einsum('gei,igo->ego', token_attention_weights.astype(jnp.float32), latent_value_rows, precision=lax.Precision.HIGHEST)
        token_attention = token_attention.reshape(row_count, D).astype(jnp.bfloat16)
        tok_mid = token_block.astype(jnp.float32) + project(token_attention, w_out_tok)
        mlp_in = (normalize(tok_mid) * mlp_gain).astype(jnp.bfloat16)
        hidden = jax.nn.gelu(project(mlp_in, w_up), approximate=False).astype(jnp.bfloat16)
        tok_out = (tok_mid + project(hidden, w_down)).astype(jnp.bfloat16)
        peak_next = jnp.maximum(peak_now, lax.optimization_barrier(jnp.max(attention_scores, axis=1)))
        column_attention_weights = jnp.exp(attention_scores - peak_next[:, None, :])
        rescale_factor = jnp.exp(peak_now - peak_next)
        total_next = total_now * rescale_factor + lax.optimization_barrier(jnp.sum(column_attention_weights, axis=1))
        token_value_rows = val_tok.astype(jnp.float32).reshape(row_count, HEADS, HEAD_DIM)
        summed_result = summed_result * jnp.transpose(rescale_factor)[:, :, None] + jnp.einsum('gti,tgb->igb', column_attention_weights, token_value_rows, precision=lax.Precision.HIGHEST)
        return ((peak_next, total_next, summed_result), tok_out)
    start_state = (jnp.full((HEADS, LATENTS), -jnp.inf, dtype=jnp.float32), jnp.zeros((HEADS, LATENTS), jnp.float32), jnp.zeros((LATENTS, HEADS, HEAD_DIM), jnp.float32))
    final_state, tok_blocks = lax.scan(advance, start_state, token_blocks)
    col_total = final_state[1]
    col_sum = final_state[2]
    lat_attn = (col_sum / jnp.transpose(col_total)[:, :, None]).reshape(LATENTS, D)
    lat_mixed = normalize(lat_attn).astype(jnp.bfloat16)
    latents_out = (latents.astype(jnp.float32) + project(lat_mixed, w_out_lat)).astype(jnp.bfloat16)
    tokens_out = tok_blocks.reshape(TOKENS, D)
    return (tokens_out, latents_out)
```

```python
import functools

import jax
import jax.numpy as jnp
from jax import lax
from jax.experimental import pallas as pl
from jax.experimental.pallas import tpu as pltpu
from jax.sharding import PartitionSpec as P

HEAD_DIM = 64
PAIR = 2 * HEAD_DIM
NORM_EPS = 1e-06
MESH = pl.DeviceIdType.MESH
F32 = jnp.float32
BF16 = jnp.bfloat16

(
    S_W, S_LAT, S_UP1, S_DOWN1, S_WOUT, S_PROJ, S_PROJ2, S_UP2, S_DOWN2, S_UP3, S_DOWN3,
    S_ATT, S_COL, S_RS, S_ZC, S_AG, S_SQ, S_PART, S_LO, S_MIN, S_MP0, S_MP1, S_RV,
) = range(23)


def scale_of(values):
    return lax.rsqrt(jnp.mean(values * values, axis=-1, keepdims=True) + NORM_EPS)


def dot(left_side, right_side):
    return jnp.dot(left_side, right_side, preferred_element_type=F32)


def gelu(values):
    return 0.5 * values * (1.0 + lax.erf(values * (0.5**0.5)))


def kernel(
    nx, ny, nz,
    tokens, latents, tok_gain, lat_gain, mlp_gain,
    w_ref_tok, w_val_tok, w_out_tok, w_ref_lat, w_val_lat, w_out_lat, w_up, w_down,
    tokens_out, latents_out,
    wtok, up, down, wlat, latx, wout, rvo, rv, lat_rv, km, vm, scores, cmax, acc, att_out, att,
    col_in, blk, rs, zb, lab, sq, sq_in, part, part_in, mid, mlp_in, hid, mp, mp_in,
    load, send, recv,
):
    ng = nx * ny
    nm = 2 * nz
    rows, width = tokens.shape
    g = lax.axis_index("group")
    m = lax.axis_index("member")
    z = lax.div(m, 2)
    c = lax.rem(m, 2)
    y = lax.div(g, nx)
    x = lax.rem(g, nx)
    other = 1 - c
    partner = (g, z * 2 + other)
    gpair = lax.div(g, 2)

    def remote(src, dst, slot, device):
        return pltpu.make_async_remote_copy(
            src_ref=src, dst_ref=dst, send_sem=send.at[min(slot, S_RV)] if isinstance(slot, int) else send.at[S_RV],
            recv_sem=recv.at[slot], device_id=device, device_id_type=MESH,
        )

    def local(src, dst, slot):
        return pltpu.make_async_copy(src, dst, recv.at[slot])

    def wait_recv(ref, slot):
        pltpu.make_async_copy(ref, ref, recv.at[slot]).wait()

    def wait_send(ref, slot):
        pltpu.make_async_copy(ref, ref, send.at[slot]).wait()

    def each(low, high, body):
        def step(i, carry):
            body(i)
            return carry

        lax.fori_loop(low, high, step, 0)

    def lanes(index, size=PAIR):
        return pl.ds(pl.multiple_of(index * size, size), size)

    def block_rows(index, size=64):
        return pl.ds(pl.multiple_of(index * size, size), size)

    loads = [
        pltpu.make_async_copy(w_ref_tok, wtok.at[0], load.at[0]),
        pltpu.make_async_copy(w_val_tok, wtok.at[1], load.at[1]),
        pltpu.make_async_copy(w_out_tok, wtok.at[2], load.at[2]),
        pltpu.make_async_copy(w_up, up.at[0], load.at[3]),
        pltpu.make_async_copy(w_down, down.at[0], load.at[4]),
    ]
    for item in loads:
        item.start()

    barrier = pltpu.get_barrier_semaphore()

    def greet(device):
        pl.semaphore_signal(barrier, inc=1, device_id=device, device_id_type=MESH)

    each(1, nm, lambda k: greet((g, lax.rem(m + k, nm))))
    each(1, ng, lambda k: greet((lax.rem(g + k, ng), m)))

    @pl.when(g != m)
    def _():
        greet((m, g))

    pl.semaphore_wait(barrier, nm + ng - 2 + (g != m).astype(jnp.int32))

    own_rows = block_rows(m)

    def send_w(k):
        zz = lax.rem(z + k, nz)
        remote(w_ref_lat.at[:, lanes(zz)], wlat.at[own_rows, :], S_W, (g, zz * 2)).start()
        remote(w_val_lat.at[:, lanes(zz)], wlat.at[own_rows, :], S_W, (g, zz * 2 + 1)).start()

    @pl.when(g != m)
    def _():
        remote(latents, latx, S_LAT, (m, g)).start()

    @pl.when(g == m)
    def _():
        local(latents, latx, S_LAT).start()

    each(1, nz, send_w)

    @pl.when(c == 0)
    def _():
        local(w_ref_lat.at[:, lanes(z)], wlat.at[own_rows, :], S_W).start()
        remote(w_val_lat.at[:, lanes(z)], wlat.at[own_rows, :], S_W, partner).start()

    @pl.when(c == 1)
    def _():
        local(w_val_lat.at[:, lanes(z)], wlat.at[own_rows, :], S_W).start()
        remote(w_ref_lat.at[:, lanes(z)], wlat.at[own_rows, :], S_W, partner).start()

    up_rows = width // ng
    down_rows = down.shape[1] // ny
    down_cols = width // nx
    up_piece = block_rows(g, up_rows)
    down_piece = (block_rows(y, down_rows), lanes(x, down_cols))

    def send_mlp(k):
        device = (g, lax.rem(z + k, nz) * 2 + c)
        remote(w_up.at[up_piece, :], up.at[nz - k, up_piece, :], S_UP1, device).start()
        remote(
            w_down.at[down_piece[0], down_piece[1]],
            down.at[nz - k, down_piece[0], down_piece[1]], S_DOWN1, device,
        ).start()

    each(1, nz, send_mlp)

    tok32 = tokens[...].astype(F32)
    tok_norm = (tok32 * scale_of(tok32) * tok_gain[...]).astype(BF16)
    loads[0].wait()
    loads[1].wait()
    for kind in range(2):
        for n in range(nz // 2):
            made = dot(tok_norm, wtok[kind, :, n * 256 : (n + 1) * 256]).astype(BF16)
            for i in range(2):
                rvo[2 * n + i, :, kind * PAIR : (kind + 1) * PAIR] = made[:, i * PAIR : (i + 1) * PAIR]
    local(rvo.at[z], rv.at[0], S_RV).start()

    def send_rv(k):
        zz = lax.rem(z + k, nz)
        remote(rvo.at[zz], rv.at[nz - k], S_RV + nz - k, (g, zz * 2 + c)).start()

    each(1, nz, send_rv)

    def send_wout(k):
        device = (g, lax.rem(z + k, nz) * 2 + c)
        remote(w_out_lat.at[:, lanes(gpair)], wout.at[block_rows(k), :], S_WOUT, device).start()

    local(w_out_lat.at[:, lanes(gpair)], wout.at[pl.ds(0, 64), :], S_WOUT).start()
    each(1, nz, send_wout)

    wait_recv(latx, S_LAT)
    lat32 = latx[...].astype(F32)
    lat_norm = (lat32 * scale_of(lat32) * lat_gain[...]).astype(BF16)
    wait_recv(wlat, S_W)
    proj_rows = block_rows(g)
    lat_rv[c, proj_rows, :] = dot(lat_norm, wlat[...]).astype(BF16)

    def send_proj(k):
        block = lat_rv.at[c, proj_rows, :]
        remote(block, block, S_PROJ, (lax.rem(g + k, ng), m)).start()

    each(1, ng, send_proj)

    wait_recv(up.at[pl.ds(1, nz - 1), up_piece, :], S_UP1)
    wait_recv(down.at[pl.ds(1, nz - 1), down_piece[0], down_piece[1]], S_DOWN1)

    def x_peer(k):
        return (y * nx + lax.rem(x + k, nx), m)

    def y_peer(k):
        return (lax.rem(y + k, ny) * nx + x, m)

    def send_up2(k):
        block = up.at[pl.ds(1, nz - 1), up_piece, :]
        remote(block, block, S_UP2, x_peer(k)).start()

    def send_down2(k):
        block = down.at[pl.ds(1, nz - 1), down_piece[0], down_piece[1]]
        remote(block, block, S_DOWN2, y_peer(k)).start()

    each(1, nx, send_up2)
    each(1, ny, send_down2)

    wait_recv(lat_rv.at[0, pl.ds(0, (ng - 1) * 64), :], S_PROJ)
    remote(lat_rv.at[c], lat_rv.at[c], S_PROJ2, partner).start()

    wait_recv(up.at[pl.ds(1, nz - 1), pl.ds(0, (nx - 1) * up_rows), :], S_UP2)
    wait_recv(down.at[pl.ds(1, nz - 1), pl.ds(0, (ny - 1) * down_rows), pl.ds(0, down_cols)], S_DOWN2)
    up_wide = block_rows(y, nx * up_rows)

    def send_up3(k):
        block = up.at[pl.ds(1, nz - 1), up_wide, :]
        remote(block, block, S_UP3, y_peer(k)).start()

    def send_down3(k):
        block = down.at[pl.ds(1, nz - 1), :, down_piece[1]]
        remote(block, block, S_DOWN3, x_peer(k)).start()

    each(1, ny, send_up3)
    each(1, nx, send_down3)

    wait_recv(lat_rv.at[other], S_PROJ2)
    lat_count = lat_rv.shape[1]
    lane = lax.broadcasted_iota(jnp.int32, (lat_count, PAIR), 1)
    keys = lat_rv[0].astype(F32) * HEAD_DIM ** (-0.5)
    values = lat_rv[1].astype(F32)
    for h in range(2):
        mine = (lane < HEAD_DIM) if h == 0 else (lane >= HEAD_DIM)
        km[h] = jnp.where(mine, keys, 0.0).astype(BF16)
        vm[h] = jnp.where(mine, values, 0.0).astype(BF16)

    cmax[...] = jnp.full(cmax.shape, -jnp.inf, F32)
    pair_lanes = lanes(z)

    def attend(i):
        half = lax.div(i + 1, 2)
        k = jnp.where(lax.rem(i, 2) == 1, half, lax.rem(nz - half, nz))
        wait_recv(rv.at[k], S_RV + k)
        query = rv[k, :, 0:PAIR]
        result = jnp.zeros((rows, PAIR), F32)
        for h in range(2):
            score = lax.dot_general(query, km[h], (((1,), (1,)), ((), ())), preferred_element_type=F32)
            scores[h, k] = score
            cmax[h] = jnp.maximum(cmax[h], jnp.max(score.reshape(rows // 8, 8, lat_count), axis=0))
            exponent = jnp.exp(score - jnp.max(score, axis=1, keepdims=True))
            inverse = 1.0 / jnp.sum(exponent, axis=1, keepdims=True)
            result = result + dot((exponent * inverse).astype(BF16), vm[h])
        att_out[k] = result.astype(BF16)

        @pl.when(i == 0)
        def _():
            local(att_out.at[0], att.at[:, pair_lanes], S_ATT).start()

        @pl.when(i > 0)
        def _():
            device = (g, lax.rem(z + k, nz) * 2 + c)
            remote(att_out.at[k], att.at[:, pair_lanes], S_ATT, device).start()

    each(0, nz, attend)

    peaks = [jnp.max(cmax[h], axis=0, keepdims=True) for h in range(2)]
    acc[...] = jnp.zeros(acc.shape, F32)

    def columns(t):
        pair = rv[pl.ds(2 * t, 2), :, PAIR : 2 * PAIR].reshape(2 * rows, PAIR)
        turned = pair.astype(F32).T.astype(BF16)
        ones = jnp.ones((16, 2 * rows), BF16)
        for h in range(2):
            score = scores[h, pl.ds(2 * t, 2)].reshape(2 * rows, lat_count)
            exponent = jnp.exp(score - peaks[h]).astype(BF16)
            left = jnp.concatenate([turned[h * HEAD_DIM : (h + 1) * HEAD_DIM], ones], axis=0)
            acc[h] = acc[h] + dot(left, exponent)

    each(0, nz // 2, columns)
    for h in range(2):
        acc[h, 72:80, :] = jnp.broadcast_to(peaks[h], (8, lat_count))
    remote(acc.at[other], col_in, S_COL, partner).start()

    wait_recv(att, S_ATT)
    loads[2].wait()
    mid[...] = tokens[...].astype(F32) + dot(att[...], wtok[2])
    mid32 = mid[...]
    mlp_in[c] = (mid32 * scale_of(mid32) * mlp_gain[...]).astype(BF16)
    remote(mlp_in.at[c], mlp_in.at[c], S_MIN, partner).start()

    wait_recv(col_in, S_COL)
    own_peak = acc[c, 72:80, :]
    in_peak = col_in[72:80, :]
    peak = jnp.maximum(own_peak, in_peak)
    own_scale = jnp.exp(own_peak - peak)
    in_scale = jnp.exp(in_peak - peak)
    own_sums = acc[c, 0:72, :].reshape(9, 8, lat_count)
    in_sums = col_in[0:72, :].reshape(9, 8, lat_count)
    sums = (own_sums * own_scale[None] + in_sums * in_scale[None]).reshape(72, lat_count)
    for b in range(ng):
        span = slice((b // 2) * PAIR, (b // 2 + 1) * PAIR)
        blk[b, 0:32, :] = sums[(b % 2) * 32 : (b % 2) * 32 + 32, span]
        blk[b, 32:40, :] = sums[64:72, span]
        blk[b, 40:48, :] = peak[:, span]

    def block_of(gg):
        return 2 * lax.rem(z + lax.div(gg, 2), nz) + lax.rem(gg, 2)

    def send_blk(k):
        gg = lax.rem(g + k, ng)
        remote(blk.at[block_of(gg)], rs.at[g], S_RS, (gg, m)).start()

    local(blk.at[block_of(g)], rs.at[g], S_RS).start()
    each(1, ng, send_blk)

    loads[3].wait()
    loads[4].wait()
    wait_recv(mlp_in.at[other], S_MIN)
    wait_recv(up.at[pl.ds(1, nz - 1), pl.ds(0, (ny - 1) * nx * up_rows), :], S_UP3)
    both = mlp_in[...].reshape(2 * rows, width)
    for n in range(nz // 2):
        piece = jnp.concatenate([up[2 * n], up[2 * n + 1]], axis=1)
        hid[:, n * 256 : (n + 1) * 256] = gelu(dot(both, piece)).astype(BF16)

    wait_recv(rs, S_RS)
    all_peaks = rs[:, 40:48, :]
    factor = jnp.exp(all_peaks - jnp.max(all_peaks, axis=0, keepdims=True))
    total = jnp.sum(rs[:, 32:40, :] * factor, axis=0)
    summed = jnp.sum(rs[:, 0:32, :].reshape(ng, 4, 8, PAIR) * factor[:, None], axis=0)
    zb[...] = (summed / total[None]).reshape(32, PAIR)
    owner = lax.rem(z + gpair, nz)

    @pl.when(owner == z)
    def _():
        local(zb, lab.at[g], S_ZC).start()

    @pl.when(owner != z)
    def _():
        remote(zb, lab.at[g], S_ZC, (g, owner * 2 + c)).start()

    wait_recv(down.at[pl.ds(1, nz - 1), :, pl.ds(0, (nx - 1) * down_cols)], S_DOWN3)
    hidden = hid[...]
    half_width = width // 2

    def mlp_out(first, last, slot):
        for n in range(first, last, min(256, half_width)):
            span = slice(n, n + min(256, half_width))
            made = dot(hidden, down[:, :, span].reshape(hidden.shape[1], min(256, half_width)))
            mp[:, :, span] = made.reshape(2, rows, min(256, half_width))
        span = pl.ds(first, last - first)
        remote(mp.at[other, :, span], mp_in.at[:, span], slot, partner).start()

    mlp_out(0, half_width, S_MP0)

    wait_recv(zb, S_ZC)

    def send_lab(k):
        remote(lab.at[g], lab.at[g], S_AG, (lax.rem(g + k, ng), m)).start()

    each(1, ng, send_lab)

    mlp_out(half_width, width, S_MP1)

    wait_recv(lab.at[pl.ds(0, ng - 1)], S_AG)
    attended = lab[...].reshape(ng * 32, PAIR)
    sq[...] = jnp.broadcast_to(jnp.sum(attended * attended, axis=0, keepdims=True), (8, PAIR))
    remote(sq, sq_in, S_SQ, partner).start()

    wait_recv(mp_in.at[:, pl.ds(0, half_width)], S_MP0)
    tokens_out[:, 0:half_width] = (
        mid[:, 0:half_width] + (mp[c, :, 0:half_width] + mp_in[:, 0:half_width])
    ).astype(BF16)

    wait_recv(sq_in, S_SQ)
    norm = lax.rsqrt((sq[0:1, :] + sq_in[0:1, :]) * (1.0 / width) + NORM_EPS)
    mixed = (attended * norm).T.astype(BF16)
    wait_recv(wout, S_WOUT)
    part[...] = dot(mixed, wout[...]).reshape(2, 64, PAIR)
    remote(part.at[other], part_in, S_PART, partner).start()

    wait_recv(mp_in.at[:, pl.ds(half_width, half_width)], S_MP1)
    tokens_out[:, half_width:width] = (
        mid[:, half_width:width] + (mp[c, :, half_width:width] + mp_in[:, half_width:width])
    ).astype(BF16)

    wait_recv(part_in, S_PART)
    own_lanes = lanes(gpair)
    latents_out[:, own_lanes] = (
        latents[:, own_lanes].astype(F32) + (part[c] + part_in[...])
    ).astype(BF16)

    def send_lo(k):
        device = (2 * lax.rem(gpair + k, nz) + lax.rem(g, 2), m)
        remote(latents_out.at[:, own_lanes], latents_out.at[:, own_lanes], S_LO, device).start()

    each(1, nz, send_lo)
    wait_recv(latents_out.at[:, pl.ds(0, (nz - 1) * PAIR)], S_LO)

    @pl.when(g != m)
    def _():
        wait_send(latx, S_LAT)

    @pl.when(owner != z)
    def _():
        wait_send(zb, S_ZC)

    wait_send(wlat.at[pl.ds(0, (nm - 1) * 64), :], S_W)
    wait_send(up.at[pl.ds(1, nz - 1), up_piece, :], S_UP1)
    wait_send(down.at[pl.ds(1, nz - 1), down_piece[0], down_piece[1]], S_DOWN1)
    wait_send(rv.at[pl.ds(1, nz - 1)], S_RV)
    wait_send(wout.at[pl.ds(0, (nz - 1) * 64), :], S_WOUT)
    wait_send(lat_rv.at[0, pl.ds(0, (ng - 1) * 64), :], S_PROJ)
    wait_send(lat_rv.at[0], S_PROJ2)
    wait_send(up.at[pl.ds(1, nz - 1), pl.ds(0, (nx - 1) * up_rows), :], S_UP2)
    wait_send(down.at[pl.ds(1, nz - 1), pl.ds(0, (ny - 1) * down_rows), pl.ds(0, down_cols)], S_DOWN2)
    wait_send(up.at[pl.ds(1, nz - 1), pl.ds(0, (ny - 1) * nx * up_rows), :], S_UP3)
    wait_send(down.at[pl.ds(1, nz - 1), :, pl.ds(0, (nx - 1) * down_cols)], S_DOWN3)
    wait_send(att_out.at[pl.ds(1, nz - 1)], S_ATT)
    wait_send(col_in, S_COL)
    wait_send(mlp_in.at[0], S_MIN)
    wait_send(rs.at[pl.ds(0, ng - 1)], S_RS)
    wait_send(lab.at[pl.ds(0, ng - 1)], S_AG)
    wait_send(sq_in, S_SQ)
    wait_send(part_in, S_PART)
    wait_send(mp_in.at[:, pl.ds(0, half_width)], S_MP0)
    wait_send(mp_in.at[:, pl.ds(half_width, half_width)], S_MP1)
    wait_send(latents_out.at[:, pl.ds(0, (nz - 1) * PAIR)], S_LO)


def per_device(nx, ny, nz, *args):
    (tokens, latents, tok_gain, lat_gain, mlp_gain, *weights) = args
    ng = nx * ny
    rows, width = tokens.shape
    lat_count = latents.shape[0] * 2 * nz
    unit = weights[6].shape[1]
    vmem = pl.BlockSpec(memory_space=pltpu.VMEM)
    anywhere = pl.BlockSpec(memory_space=pl.ANY)
    scratch = [
        ((3, width, width), BF16),
        ((nz, width, unit), BF16),
        ((nz, unit, width), BF16),
        ((width, PAIR), BF16),
        ((64, width), BF16),
        ((nz * 64, PAIR), BF16),
        ((nz, rows, 2 * PAIR), BF16),
        ((nz, rows, 2 * PAIR), BF16),
        ((2, lat_count, PAIR), BF16),
        ((2, lat_count, PAIR), BF16),
        ((2, lat_count, PAIR), BF16),
        ((2, nz, rows, lat_count), F32),
        ((2, 8, lat_count), F32),
        ((2, 80, lat_count), F32),
        ((nz, rows, PAIR), BF16),
        ((rows, width), BF16),
        ((80, lat_count), F32),
        ((ng, 48, PAIR), F32),
        ((ng, 48, PAIR), F32),
        ((32, PAIR), F32),
        ((ng, 32, PAIR), F32),
        ((8, PAIR), F32),
        ((8, PAIR), F32),
        ((2, 64, PAIR), F32),
        ((64, PAIR), F32),
        ((rows, width), F32),
        ((2, rows, width), BF16),
        ((2 * rows, nz * unit), BF16),
        ((2, rows, width), F32),
        ((rows, width), F32),
    ]
    return pl.pallas_call(
        functools.partial(kernel, nx, ny, nz),
        out_shape=(
            jax.ShapeDtypeStruct(tokens.shape, BF16),
            jax.ShapeDtypeStruct(latents.shape, BF16),
        ),
        in_specs=[vmem] * 5 + [anywhere] * 8,
        out_specs=(vmem, vmem),
        scratch_shapes=[pltpu.VMEM(shape, kind) for shape, kind in scratch]
        + [
            pltpu.SemaphoreType.DMA((5,)),
            pltpu.SemaphoreType.DMA((S_RV + 1,)),
            pltpu.SemaphoreType.DMA((S_RV + nz,)),
        ],
        compiler_params=pltpu.CompilerParams(
            collective_id=0, has_side_effects=True, vmem_limit_bytes=56 * 1024 * 1024
        ),
        name="layer",
    )(
        tokens,
        latents,
        tok_gain.reshape(1, width),
        lat_gain.reshape(1, width),
        mlp_gain.reshape(1, width),
        *weights,
    )


def solution(mesh):
    ng = mesh.shape["group"]
    nz = mesh.shape["member"] // 2
    nx = int(round(ng**0.5))
    in_specs = (
        P(("group", "member"), None),
        P("member", None),
        P(),
        P(),
        P(),
        P(),
        P(),
        P(),
        P("member", None),
        P("member", None),
        P("member", None),
        P(None, "member"),
        P("member", None),
    )
    out_specs = (P(("group", "member"), None), P("member", None))
    return jax.shard_map(
        functools.partial(per_device, nx, ng // nx, nz),
        mesh=mesh, in_specs=in_specs, out_specs=out_specs, check_vma=False,
    )
```

```python
import functools

import jax
import jax.numpy as jnp
from jax import lax
from jax.experimental import pallas as pl
from jax.experimental.pallas import tpu as pltpu
from jax.sharding import PartitionSpec as P

HEAD_DIM = 64
PAIR = 2 * HEAD_DIM
NORM_EPS = 1e-06
MESH = pl.DeviceIdType.MESH
F32 = jnp.float32
BF16 = jnp.bfloat16

(
    S_W, S_W2, S_LAT, S_UP1, S_DOWN1, S_WOUT, S_VAL, S_PROJ, S_PROJ2, S_ATT, S_COL, S_RS, S_ZC, S_AG,
    S_SQ, S_PART, S_LO, S_MIN, S_MP0, S_MP1,
) = range(20)
S_RING = 20
S_REF = 36


def scale_of(values):
    return lax.rsqrt(jnp.mean(values * values, axis=-1, keepdims=True) + NORM_EPS)


def dot(left_side, right_side):
    return jnp.dot(left_side, right_side, preferred_element_type=F32)


def gelu(values):
    return 0.5 * values * (1.0 + lax.erf(values * (0.5**0.5)))


def kernel(
    nx, ny, nz,
    tokens, latents, tok_gain, lat_gain, mlp_gain,
    w_ref_tok, w_val_tok, w_out_tok, w_ref_lat, w_val_lat, w_out_lat, w_up, w_down,
    tokens_out, latents_out,
    wtok, up, down, wlat, latx, wout, rvo, rv, lat_rv, km, vm, scores, cmax, acc, att_out, att,
    col_in, blk, rs, zb, lab, sq, sq_in, part, part_in, mid, mlp_in, hid, mp, mp_in,
    load, send, recv,
):
    ng = nx * ny
    nm = 2 * nz
    rows, width = tokens.shape
    g = lax.axis_index("group")
    m = lax.axis_index("member")
    z = lax.div(m, 2)
    c = lax.rem(m, 2)
    y = lax.div(g, nx)
    x = lax.rem(g, nx)
    other = 1 - c
    partner = (g, z * 2 + other)
    gpair = lax.div(g, 2)

    def remote(src, dst, slot, device):
        return pltpu.make_async_remote_copy(
            src_ref=src, dst_ref=dst, send_sem=send.at[min(slot, S_REF)] if isinstance(slot, int) else send.at[S_REF],
            recv_sem=recv.at[slot], device_id=device, device_id_type=MESH,
        )

    def local(src, dst, slot):
        return pltpu.make_async_copy(src, dst, recv.at[slot])

    def wait_recv(ref, slot):
        pltpu.make_async_copy(ref, ref, recv.at[slot]).wait()

    def wait_send(ref, slot):
        pltpu.make_async_copy(ref, ref, send.at[slot]).wait()

    def each(low, high, body):
        def step(i, carry):
            body(i)
            return carry

        lax.fori_loop(low, high, step, 0)

    def lanes(index, size=PAIR):
        return pl.ds(pl.multiple_of(index * size, size), size)

    def block_rows(index, size=64):
        return pl.ds(pl.multiple_of(index * size, size), size)

    loads = [
        pltpu.make_async_copy(w_ref_tok, wtok.at[0], load.at[0]),
        pltpu.make_async_copy(w_val_tok, wtok.at[1], load.at[1]),
        pltpu.make_async_copy(w_out_tok, wtok.at[2], load.at[2]),
        pltpu.make_async_copy(w_up, up.at[0], load.at[3]),
        pltpu.make_async_copy(w_down, down.at[0], load.at[4]),
    ]
    for item in loads:
        item.start()

    barrier = pltpu.get_barrier_semaphore()

    def greet(device):
        pl.semaphore_signal(barrier, inc=1, device_id=device, device_id_type=MESH)

    owner = lax.rem(z + gpair, nz)

    each(1, nm, lambda k: greet((g, lax.rem(m + k, nm))))
    each(1, ng, lambda k: greet((lax.rem(g + k, ng), m)))
    tok32 = tokens[...].astype(F32)
    tok_norm = (tok32 * scale_of(tok32) * tok_gain[...]).astype(BF16)

    def project_tokens(kind):
        for n in range(nz // 2):
            made = dot(tok_norm, wtok[kind, :, n * 256 : (n + 1) * 256]).astype(BF16)
            for i in range(2):
                rvo[kind, 2 * n + i] = made[:, i * PAIR : (i + 1) * PAIR]

    loads[0].wait()
    project_tokens(0)
    pl.semaphore_wait(barrier, nm + ng - 2)

    piece_rows = 64 // nx
    x_rows = block_rows(x, piece_rows)

    def send_w(k):
        zz = lax.rem(z + k, nz)
        remote(w_ref_lat.at[x_rows, lanes(zz)], wlat.at[m, x], S_W, (g, zz * 2)).start()
        remote(w_val_lat.at[x_rows, lanes(zz)], wlat.at[m, x], S_W, (g, zz * 2 + 1)).start()

    each(1, nz, send_w)

    @pl.when(c == 0)
    def _():
        local(w_ref_lat.at[x_rows, lanes(z)], wlat.at[m, x], S_W).start()
        remote(w_val_lat.at[x_rows, lanes(z)], wlat.at[m, x], S_W, partner).start()

    @pl.when(c == 1)
    def _():
        local(w_val_lat.at[x_rows, lanes(z)], wlat.at[m, x], S_W).start()
        remote(w_ref_lat.at[x_rows, lanes(z)], wlat.at[m, x], S_W, partner).start()

    high = nz // ny
    z_low = lax.rem(z, ny)
    z_high = lax.div(z, ny)
    for hh in range(high):
        zz = lax.rem(z_low + ny - y, ny) + ny * hh
        for cc in range(2):
            to_self = (zz == z) & (c == cc)

            @pl.when(to_self)
            def _():
                local(latents.at[x_rows, :], latx.at[z_high, c], S_LAT).start()

            @pl.when(jnp.logical_not(to_self))
            def _(zz=zz, cc=cc):
                remote(latents.at[x_rows, :], latx.at[z_high, c], S_LAT, (g, zz * 2 + cc)).start()

    up_rows = width // ng
    down_rows = down.shape[1] // ny
    down_cols = width // nx
    up_piece = block_rows(g, up_rows)
    down_piece = (block_rows(y, down_rows), lanes(x, down_cols))

    def send_mlp(k):
        device = (g, lax.rem(z + k, nz) * 2 + c)
        remote(w_up.at[up_piece, :], up.at[nz - k, up_piece, :], S_UP1, device).start()
        remote(
            w_down.at[down_piece[0], down_piece[1]],
            down.at[nz - k, down_piece[0], down_piece[1]], S_DOWN1, device,
        ).start()

    local(rvo.at[0, z], rv.at[0, 0], S_REF).start()

    def send_ref(k):
        zz = lax.rem(z + k, nz)
        remote(rvo.at[0, zz], rv.at[0, nz - k], S_REF + nz - k, (g, zz * 2 + c)).start()

    each(1, nz, send_ref)
    each(1, nz, send_mlp)

    def x_peer(k):
        return (y * nx + lax.rem(x + k, nx), m)

    def y_peer(k):
        return (lax.rem(y + k, ny) * nx + x, m)

    wait_recv(wlat.at[:, x], S_W)
    each(1, nx, lambda k: remote(wlat.at[:, x], wlat.at[:, x], S_W2, x_peer(k)).start())

    loads[1].wait()
    project_tokens(1)
    local(rvo.at[1, z], rv.at[1, 0], S_VAL).start()

    def send_val(k):
        zz = lax.rem(z + k, nz)
        remote(rvo.at[1, zz], rv.at[1, nz - k], S_VAL, (g, zz * 2 + c)).start()

    each(1, nz, send_val)

    def send_wout(k):
        device = (g, lax.rem(z + k, nz) * 2 + c)
        remote(w_out_lat.at[:, lanes(gpair)], wout.at[block_rows(k), :], S_WOUT, device).start()

    wait_recv(latx, S_LAT)
    lat32 = latx[...].reshape(64, width).astype(F32)
    lat_norm = (lat32 * scale_of(lat32) * lat_gain[...]).astype(BF16)
    wait_recv(wlat.at[:, pl.ds(0, nx - 1)], S_W2)
    made = dot(lat_norm, wlat[...].reshape(width, PAIR)).astype(BF16).reshape(high, 2, piece_rows, PAIR)
    low = lax.rem(z + y, ny)
    for hh in range(high):
        for cc in range(2):
            lat_rv[c, hh, low, cc, x] = made[hh, cc]

    def send_proj(k):
        block = lat_rv.at[c, :, low, :, x]
        remote(block, block, S_PROJ, (lax.rem(g + k, ng), m)).start()

    each(1, ng, send_proj)

    local(w_out_lat.at[:, lanes(gpair)], wout.at[pl.ds(0, 64), :], S_WOUT).start()
    each(1, nz, send_wout)

    rest = pl.ds(1, nz - 1)

    def up_x(index, part, parts):
        size = up_rows // parts
        return up.at[rest, block_rows((y * nx + index) * parts + part, size), :]

    def up_y(index, part, parts):
        size = nx * up_rows // parts
        return up.at[rest, block_rows(index * parts + part, size), :]

    def down_y(index, part, parts):
        size = down_rows // parts
        return down.at[rest, block_rows(index * parts + part, size), lanes(x, down_cols)]

    def down_x(index, part, parts):
        return down.at[rest, :, lanes(index * parts + part, down_cols // parts)]

    rings = {
        "ux": (nx, x, x_peer, up_x, S_RING),
        "dy": (ny, y, y_peer, down_y, S_RING + 4),
        "uy": (ny, y, y_peer, up_y, S_RING + 8),
        "dx": (nx, x, x_peer, down_x, S_RING + 12),
    }

    def ring_start(name):
        n, at, peer, block, slot = rings[name]
        for k in sorted({1, n - 1} - {0}):
            own = block(at, 0, 1)
            remote(own, own, slot + (k != 1), peer(k)).start()

    def ring_turn(name):
        n, at, peer, block, slot = rings[name]
        if n > 1:
            wait_recv(block(at, 0, 1), slot)
        if n == 4:
            left = block(lax.rem(at + 3, 4), 0, 2)
            remote(left, left, slot + 2, peer(1)).start()
            wait_recv(block(at, 0, 1), slot + 1)
            right = block(lax.rem(at + 1, 4), 1, 2)
            remote(right, right, slot + 3, peer(3)).start()

    def ring_end(name):
        n, at, peer, block, slot = rings[name]
        if n == 4:
            wait_recv(block(at, 0, 2), slot + 2)
            wait_recv(block(at, 0, 2), slot + 3)

    def ring_sent(name):
        n, at, peer, block, slot = rings[name]
        for k in sorted({1, n - 1} - {0}):
            wait_send(block(at, 0, 1), slot + (k != 1))
        if n == 4:
            wait_send(block(at, 0, 2), slot + 2)
            wait_send(block(at, 0, 2), slot + 3)

    wait_recv(up.at[rest, up_piece, :], S_UP1)
    wait_recv(down.at[rest, down_piece[0], down_piece[1]], S_DOWN1)
    ring_start("ux")
    ring_start("dy")

    others = lat_rv.at[0].reshape(ng * 64, PAIR).at[pl.ds(0, (ng - 1) * 64), :]
    wait_recv(others, S_PROJ)
    remote(lat_rv.at[c], lat_rv.at[c], S_PROJ2, partner).start()
    ring_turn("ux")
    ring_turn("dy")

    wait_recv(lat_rv.at[other], S_PROJ2)
    lat_count = ng * 64
    lane = lax.broadcasted_iota(jnp.int32, (lat_count, PAIR), 1)
    keys = lat_rv[0].reshape(lat_count, PAIR).astype(F32) * HEAD_DIM ** (-0.5)
    values = lat_rv[1].reshape(lat_count, PAIR).astype(F32)
    for h in range(2):
        mine = (lane < HEAD_DIM) if h == 0 else (lane >= HEAD_DIM)
        km[h] = jnp.where(mine, keys, 0.0).astype(BF16)
        vm[h] = jnp.where(mine, values, 0.0).astype(BF16)

    ring_end("ux")
    ring_end("dy")
    ring_start("uy")
    ring_start("dx")

    cmax[...] = jnp.full(cmax.shape, -jnp.inf, F32)
    pair_lanes = lanes(z)

    def place(i):
        half = lax.div(i + 1, 2)
        return jnp.where(lax.rem(i, 2) == 1, half, lax.rem(nz - half, nz))

    def score_block(i):
        k = place(i)
        wait_recv(rv.at[0, k], S_REF + k)
        query = rv[0, k]
        for h in range(2):
            score = lax.dot_general(query, km[h], (((1,), (1,)), ((), ())), preferred_element_type=F32)
            scores[h, k] = score
            cmax[h] = jnp.maximum(cmax[h], jnp.max(score.reshape(rows // 8, 8, lat_count), axis=0))

    each(0, nz, score_block)

    peaks = [jnp.max(cmax[h], axis=0, keepdims=True) for h in range(2)]
    acc[...] = jnp.zeros(acc.shape, F32)
    wait_recv(rv.at[1], S_VAL)

    def columns(t):
        pair = rv[1, pl.ds(2 * t, 2)].reshape(2 * rows, PAIR)
        turned = pair.astype(F32).T.astype(BF16)
        ones = jnp.ones((16, 2 * rows), BF16)
        for h in range(2):
            score = scores[h, pl.ds(2 * t, 2)].reshape(2 * rows, lat_count)
            exponent = jnp.exp(score - peaks[h]).astype(BF16)
            left = jnp.concatenate([turned[h * HEAD_DIM : (h + 1) * HEAD_DIM], ones], axis=0)
            acc[h] = acc[h] + dot(left, exponent)

    each(0, nz // 2, columns)
    for h in range(2):
        acc[h, 72:80, :] = jnp.broadcast_to(peaks[h], (8, lat_count))
    remote(acc.at[other], col_in, S_COL, partner).start()
    ring_turn("uy")
    ring_turn("dx")

    def attend(i):
        k = place(nz - 1 - i)
        result = jnp.zeros((rows, PAIR), F32)
        for h in range(2):
            score = scores[h, k]
            exponent = jnp.exp(score - jnp.max(score, axis=1, keepdims=True))
            inverse = 1.0 / jnp.sum(exponent, axis=1, keepdims=True)
            result = result + dot((exponent * inverse).astype(BF16), vm[h])
        att_out[k] = result.astype(BF16)

        @pl.when(k == 0)
        def _():
            local(att_out.at[0], att.at[:, pair_lanes], S_ATT).start()

        @pl.when(k > 0)
        def _():
            device = (g, lax.rem(z + k, nz) * 2 + c)
            remote(att_out.at[k], att.at[:, pair_lanes], S_ATT, device).start()

    each(0, nz // 4, attend)

    wait_recv(col_in, S_COL)
    own_peak = acc[c, 72:80, :]
    in_peak = col_in[72:80, :]
    peak = jnp.maximum(own_peak, in_peak)
    own_scale = jnp.exp(own_peak - peak)
    in_scale = jnp.exp(in_peak - peak)
    own_sums = acc[c, 0:72, :].reshape(9, 8, lat_count)
    in_sums = col_in[0:72, :].reshape(9, 8, lat_count)
    sums = (own_sums * own_scale[None] + in_sums * in_scale[None]).reshape(72, lat_count)
    for b in range(ng):
        span = slice((b // 2) * PAIR, (b // 2 + 1) * PAIR)
        blk[b, 0:32, :] = sums[(b % 2) * 32 : (b % 2) * 32 + 32, span]
        blk[b, 32:36, :] = sums[64:68, span]
        blk[b, 36:40, :] = peak[0:4, span]

    def block_of(gg):
        return 2 * lax.rem(z + lax.div(gg, 2), nz) + lax.rem(gg, 2)

    def send_blk(k):
        gg = lax.rem(g + k, ng)
        remote(blk.at[block_of(gg)], rs.at[g], S_RS, (gg, m)).start()

    local(blk.at[block_of(g)], rs.at[g], S_RS).start()
    each(1, ng, send_blk)

    each(nz // 4, nz, attend)

    wait_recv(rs, S_RS)
    all_peaks = rs[:, 36:37, :]
    factor = jnp.exp(all_peaks - jnp.max(all_peaks, axis=0, keepdims=True))
    total = jnp.sum(rs[:, 32:33, :] * factor, axis=0)
    summed = jnp.sum(rs[:, 0:32, :] * factor, axis=0)
    zb[...] = summed / total

    @pl.when(owner == z)
    def _():
        local(zb, lab.at[g], S_ZC).start()

    @pl.when(owner != z)
    def _():
        remote(zb, lab.at[g], S_ZC, (g, owner * 2 + c)).start()

    wait_recv(att, S_ATT)
    loads[2].wait()
    mid[...] = tokens[...].astype(F32) + dot(att[...], wtok[2])
    mid32 = mid[...]
    mlp_in[c] = (mid32 * scale_of(mid32) * mlp_gain[...]).astype(BF16)
    remote(mlp_in.at[c], mlp_in.at[c], S_MIN, partner).start()

    wait_recv(zb, S_ZC)

    def send_lab(k):
        remote(lab.at[g], lab.at[g], S_AG, (lax.rem(g + k, ng), m)).start()

    each(1, ng, send_lab)

    loads[3].wait()
    loads[4].wait()
    wait_recv(mlp_in.at[other], S_MIN)
    ring_end("uy")
    both = mlp_in[...].reshape(2 * rows, width)
    for n in range(nz // 2):
        piece = jnp.concatenate([up[2 * n], up[2 * n + 1]], axis=1)
        hid[:, n * 256 : (n + 1) * 256] = gelu(dot(both, piece)).astype(BF16)

    wait_recv(lab.at[pl.ds(0, ng - 1)], S_AG)
    attended = lab[...].reshape(ng * 32, PAIR)
    sq[...] = jnp.broadcast_to(jnp.sum(attended * attended, axis=0, keepdims=True), (8, PAIR))
    remote(sq, sq_in, S_SQ, partner).start()

    ring_end("dx")
    half_width = width // 2
    step = min(256, half_width)

    def mlp_out(first, last, slot):
        for n in range(first, last, step):
            span = slice(n, n + step)
            made = dot(hid[...], down[:, :, span].reshape(hid.shape[1], step))
            mp[:, :, span] = made.reshape(2, rows, step)
        span = pl.ds(first, last - first)
        remote(mp.at[other, :, span], mp_in.at[:, span], slot, partner).start()

    mlp_out(0, half_width, S_MP0)

    wait_recv(sq_in, S_SQ)
    norm = lax.rsqrt((sq[0:1, :] + sq_in[0:1, :]) * (1.0 / width) + NORM_EPS)
    mixed = (attended * norm).T.astype(BF16)
    wait_recv(wout, S_WOUT)
    part[...] = dot(mixed, wout[...]).reshape(2, 64, PAIR)
    remote(part.at[other], part_in, S_PART, partner).start()

    mlp_out(half_width, width, S_MP1)

    wait_recv(part_in, S_PART)
    own_lanes = lanes(gpair)
    latents_out[:, own_lanes] = (
        latents[:, own_lanes].astype(F32) + (part[c] + part_in[...])
    ).astype(BF16)

    def send_lo(k):
        device = (2 * lax.rem(gpair + k, nz) + lax.rem(g, 2), m)
        remote(latents_out.at[:, own_lanes], latents_out.at[:, own_lanes], S_LO, device).start()

    each(1, nz, send_lo)

    for first, slot in ((0, S_MP0), (half_width, S_MP1)):
        span = slice(first, first + half_width)
        wait_recv(mp_in.at[:, pl.ds(first, half_width)], slot)
        tokens_out[:, span] = (mid[:, span] + (mp[c, :, span] + mp_in[:, span])).astype(BF16)

    wait_recv(latents_out.at[:, pl.ds(0, (nz - 1) * PAIR)], S_LO)

    @pl.when(y != 0)
    def _():
        wait_send(latx.at[0, 0], S_LAT)

    for _ in range(2 * high - 1):
        wait_send(latx.at[0, 0], S_LAT)

    @pl.when(owner != z)
    def _():
        wait_send(zb, S_ZC)

    wait_send(lab.at[pl.ds(0, ng - 1)], S_AG)
    wait_send(wlat.at[pl.ds(0, nm - 1), 0], S_W)
    wait_send(wlat.at[:, pl.ds(0, nx - 1)], S_W2)
    wait_send(up.at[rest, up_piece, :], S_UP1)
    wait_send(down.at[rest, down_piece[0], down_piece[1]], S_DOWN1)
    wait_send(rv.at[0, rest], S_REF)
    wait_send(rv.at[1, rest], S_VAL)
    wait_send(wout.at[pl.ds(0, (nz - 1) * 64), :], S_WOUT)
    wait_send(others, S_PROJ)
    wait_send(lat_rv.at[0], S_PROJ2)
    for name in rings:
        ring_sent(name)
    wait_send(att_out.at[pl.ds(1, nz - 1)], S_ATT)
    wait_send(col_in, S_COL)
    wait_send(mlp_in.at[0], S_MIN)
    wait_send(rs.at[pl.ds(0, ng - 1)], S_RS)
    wait_send(sq_in, S_SQ)
    wait_send(part_in, S_PART)
    wait_send(mp_in.at[:, pl.ds(0, half_width)], S_MP0)
    wait_send(mp_in.at[:, pl.ds(half_width, half_width)], S_MP1)
    wait_send(latents_out.at[:, pl.ds(0, (nz - 1) * PAIR)], S_LO)


def per_device(nx, ny, nz, *args):
    (tokens, latents, tok_gain, lat_gain, mlp_gain, *weights) = args
    ng = nx * ny
    rows, width = tokens.shape
    lat_count = latents.shape[0] * 2 * nz
    unit = weights[6].shape[1]
    vmem = pl.BlockSpec(memory_space=pltpu.VMEM)
    anywhere = pl.BlockSpec(memory_space=pl.ANY)
    scratch = [
        ((3, width, width), BF16),
        ((nz, width, unit), BF16),
        ((nz, unit, width), BF16),
        ((2 * nz, nx, 64 // nx, PAIR), BF16),
        ((nz // ny, 2, 64 // nx, width), BF16),
        ((nz * 64, PAIR), BF16),
        ((2, nz, rows, PAIR), BF16),
        ((2, nz, rows, PAIR), BF16),
        ((2, nz // ny, ny, 2, nx, 64 // nx, PAIR), BF16),
        ((2, lat_count, PAIR), BF16),
        ((2, lat_count, PAIR), BF16),
        ((2, nz, rows, lat_count), F32),
        ((2, 8, lat_count), F32),
        ((2, 80, lat_count), F32),
        ((nz, rows, PAIR), BF16),
        ((rows, width), BF16),
        ((80, lat_count), F32),
        ((ng, 40, PAIR), F32),
        ((ng, 40, PAIR), F32),
        ((32, PAIR), F32),
        ((ng, 32, PAIR), F32),
        ((8, PAIR), F32),
        ((8, PAIR), F32),
        ((2, 64, PAIR), F32),
        ((64, PAIR), F32),
        ((rows, width), F32),
        ((2, rows, width), BF16),
        ((2 * rows, nz * unit), BF16),
        ((2, rows, width), F32),
        ((rows, width), F32),
    ]
    return pl.pallas_call(
        functools.partial(kernel, nx, ny, nz),
        out_shape=(
            jax.ShapeDtypeStruct(tokens.shape, BF16),
            jax.ShapeDtypeStruct(latents.shape, BF16),
        ),
        in_specs=[vmem] * 5 + [anywhere] * 8,
        out_specs=(vmem, vmem),
        scratch_shapes=[pltpu.VMEM(shape, kind) for shape, kind in scratch]
        + [
            pltpu.SemaphoreType.DMA((5,)),
            pltpu.SemaphoreType.DMA((S_REF + 1,)),
            pltpu.SemaphoreType.DMA((S_REF + nz,)),
        ],
        compiler_params=pltpu.CompilerParams(
            collective_id=0, has_side_effects=True, vmem_limit_bytes=56 * 1024 * 1024
        ),
        name="layer",
    )(
        tokens,
        latents,
        tok_gain.reshape(1, width),
        lat_gain.reshape(1, width),
        mlp_gain.reshape(1, width),
        *weights,
    )


def solution(mesh):
    ng = mesh.shape["group"]
    nz = mesh.shape["member"] // 2
    nx = int(round(ng**0.5))
    in_specs = (
        P(("group", "member"), None),
        P("member", None),
        P(),
        P(),
        P(),
        P(),
        P(),
        P(),
        P("member", None),
        P("member", None),
        P("member", None),
        P(None, "member"),
        P("member", None),
    )
    out_specs = (P(("group", "member"), None), P("member", None))
    return jax.shard_map(
        functools.partial(per_device, nx, ng // nx, nz),
        mesh=mesh, in_specs=in_specs, out_specs=out_specs, check_vma=False,
    )
```

```python
import functools

import jax
import jax.numpy as jnp
from jax import lax
from jax.experimental import pallas as pl
from jax.experimental.pallas import tpu as pltpu
from jax.sharding import PartitionSpec as P

HEAD_DIM = 64
PAIR = 2 * HEAD_DIM
NORM_EPS = 1e-06
MESH = pl.DeviceIdType.MESH
F32 = jnp.float32
BF16 = jnp.bfloat16

(
    S_W, S_W2, S_LAT, S_UP1, S_DOWN1, S_WOUT, S_VAL, S_PROJ, S_PROJ2, S_ATT, S_COL, S_RS, S_ZC, S_AG,
    S_SQ, S_PART, S_LO, S_MIN, S_MP0, S_MP1,
) = range(20)
S_RING = 20
S_REF = 36


def scale_of(values):
    return lax.rsqrt(jnp.mean(values * values, axis=-1, keepdims=True) + NORM_EPS)


def dot(left_side, right_side):
    return jnp.dot(left_side, right_side, preferred_element_type=F32)


def gelu(values):
    return 0.5 * values * (1.0 + lax.erf(values * (0.5**0.5)))


def kernel(
    nx, ny, nz,
    tokens, latents, tok_gain, lat_gain, mlp_gain,
    w_ref_tok, w_val_tok, w_out_tok, w_ref_lat, w_val_lat, w_out_lat, w_up, w_down,
    tokens_out, latents_out,
    wtok, up, down, wlat, latx, wout, rvo, rv, lat_rv, km, vm, scores, cmax, acc, att_out, att,
    col_in, blk, rs, zb, lab, sq, sq_in, part, part_in, mid, mlp_in, hid, mp, mp_in,
    load, send, recv,
):
    ng = nx * ny
    nm = 2 * nz
    rows, width = tokens.shape
    g = lax.axis_index("group")
    m = lax.axis_index("member")
    z = lax.div(m, 2)
    c = lax.rem(m, 2)
    y = lax.div(g, nx)
    x = lax.rem(g, nx)
    other = 1 - c
    partner = (g, z * 2 + other)
    gpair = lax.div(g, 2)

    def remote(src, dst, slot, device):
        return pltpu.make_async_remote_copy(
            src_ref=src, dst_ref=dst, send_sem=send.at[min(slot, S_REF)] if isinstance(slot, int) else send.at[S_REF],
            recv_sem=recv.at[slot], device_id=device, device_id_type=MESH,
        )

    def local(src, dst, slot):
        return pltpu.make_async_copy(src, dst, recv.at[slot])

    def wait_recv(ref, slot):
        pltpu.make_async_copy(ref, ref, recv.at[slot]).wait()

    def wait_send(ref, slot):
        pltpu.make_async_copy(ref, ref, send.at[slot]).wait()

    def each(low, high, body):
        def step(i, carry):
            body(i)
            return carry

        lax.fori_loop(low, high, step, 0)

    def lanes(index, size=PAIR):
        return pl.ds(pl.multiple_of(index * size, size), size)

    def block_rows(index, size=64):
        return pl.ds(pl.multiple_of(index * size, size), size)

    loads = [
        pltpu.make_async_copy(w_ref_tok, wtok.at[0], load.at[0]),
        pltpu.make_async_copy(w_val_tok, wtok.at[1], load.at[1]),
        pltpu.make_async_copy(w_out_tok, wtok.at[2], load.at[2]),
        pltpu.make_async_copy(w_up, up.at[0], load.at[3]),
        pltpu.make_async_copy(w_down, down.at[0], load.at[4]),
    ]
    for item in loads:
        item.start()

    barrier = pltpu.get_barrier_semaphore()

    def greet(device):
        pl.semaphore_signal(barrier, inc=1, device_id=device, device_id_type=MESH)

    owner = lax.rem(z + gpair, nz)

    each(1, nm, lambda k: greet((g, lax.rem(m + k, nm))))
    each(1, ng, lambda k: greet((lax.rem(g + k, ng), m)))
    tok32 = tokens[...].astype(F32)
    tok_norm = (tok32 * scale_of(tok32) * tok_gain[...]).astype(BF16)

    def project_tokens(kind):
        for n in range(nz // 2):
            made = dot(tok_norm, wtok[kind, :, n * 256 : (n + 1) * 256]).astype(BF16)
            for i in range(2):
                rvo[kind, 2 * n + i] = made[:, i * PAIR : (i + 1) * PAIR]

    loads[0].wait()
    project_tokens(0)
    pl.semaphore_wait(barrier, nm + ng - 2)

    piece_rows = 64 // nx
    x_rows = block_rows(x, piece_rows)

    def send_w(k):
        zz = lax.rem(z + k, nz)
        remote(w_ref_lat.at[x_rows, lanes(zz)], wlat.at[m, x], S_W, (g, zz * 2)).start()
        remote(w_val_lat.at[x_rows, lanes(zz)], wlat.at[m, x], S_W, (g, zz * 2 + 1)).start()

    each(1, nz, send_w)

    @pl.when(c == 0)
    def _():
        local(w_ref_lat.at[x_rows, lanes(z)], wlat.at[m, x], S_W).start()
        remote(w_val_lat.at[x_rows, lanes(z)], wlat.at[m, x], S_W, partner).start()

    @pl.when(c == 1)
    def _():
        local(w_val_lat.at[x_rows, lanes(z)], wlat.at[m, x], S_W).start()
        remote(w_ref_lat.at[x_rows, lanes(z)], wlat.at[m, x], S_W, partner).start()

    high = nz // ny
    z_low = lax.rem(z, ny)
    z_high = lax.div(z, ny)
    for hh in range(high):
        zz = lax.rem(z_low + ny - y, ny) + ny * hh
        for cc in range(2):
            to_self = (zz == z) & (c == cc)

            @pl.when(to_self)
            def _():
                local(latents.at[x_rows, :], latx.at[z_high, c], S_LAT).start()

            @pl.when(jnp.logical_not(to_self))
            def _(zz=zz, cc=cc):
                remote(latents.at[x_rows, :], latx.at[z_high, c], S_LAT, (g, zz * 2 + cc)).start()

    up_rows = width // ng
    down_rows = down.shape[1] // ny
    down_cols = width // nx
    up_piece = block_rows(g, up_rows)
    down_piece = (block_rows(y, down_rows), lanes(x, down_cols))

    def send_mlp(k):
        device = (g, lax.rem(z + k, nz) * 2 + c)
        remote(w_up.at[up_piece, :], up.at[nz - k, up_piece, :], S_UP1, device).start()
        remote(
            w_down.at[down_piece[0], down_piece[1]],
            down.at[nz - k, down_piece[0], down_piece[1]], S_DOWN1, device,
        ).start()

    each(1, nz, send_mlp)
    local(rvo.at[0, z], rv.at[0, 0], S_REF).start()

    def send_ref(k):
        zz = lax.rem(z + k, nz)
        remote(rvo.at[0, zz], rv.at[0, nz - k], S_REF + nz - k, (g, zz * 2 + c)).start()

    each(1, nz, send_ref)

    def x_peer(k):
        return (y * nx + lax.rem(x + k, nx), m)

    def y_peer(k):
        return (lax.rem(y + k, ny) * nx + x, m)

    wait_recv(wlat.at[:, x], S_W)
    each(1, nx, lambda k: remote(wlat.at[:, x], wlat.at[:, x], S_W2, x_peer(k)).start())

    loads[1].wait()
    project_tokens(1)
    local(rvo.at[1, z], rv.at[1, 0], S_VAL).start()

    def send_val(k):
        zz = lax.rem(z + k, nz)
        remote(rvo.at[1, zz], rv.at[1, nz - k], S_VAL, (g, zz * 2 + c)).start()

    each(1, nz, send_val)

    def send_wout(k):
        device = (g, lax.rem(z + k, nz) * 2 + c)
        remote(w_out_lat.at[:, lanes(gpair)], wout.at[block_rows(k), :], S_WOUT, device).start()

    wait_recv(latx, S_LAT)
    lat32 = latx[...].reshape(64, width).astype(F32)
    lat_norm = (lat32 * scale_of(lat32) * lat_gain[...]).astype(BF16)
    wait_recv(wlat.at[:, pl.ds(0, nx - 1)], S_W2)
    made = dot(lat_norm, wlat[...].reshape(width, PAIR)).astype(BF16).reshape(high, 2, piece_rows, PAIR)
    low = lax.rem(z + y, ny)
    for hh in range(high):
        for cc in range(2):
            lat_rv[c, hh, low, cc, x] = made[hh, cc]

    def send_proj(k):
        block = lat_rv.at[c, :, low, :, x]
        remote(block, block, S_PROJ, (lax.rem(g + k, ng), m)).start()

    each(1, ng, send_proj)

    local(w_out_lat.at[:, lanes(gpair)], wout.at[pl.ds(0, 64), :], S_WOUT).start()
    each(1, nz, send_wout)

    rest = pl.ds(1, nz - 1)

    def up_x(index, part, parts):
        size = up_rows // parts
        return up.at[rest, block_rows((y * nx + index) * parts + part, size), :]

    def up_y(index, part, parts):
        size = nx * up_rows // parts
        return up.at[rest, block_rows(index * parts + part, size), :]

    def down_y(index, part, parts):
        size = down_rows // parts
        return down.at[rest, block_rows(index * parts + part, size), lanes(x, down_cols)]

    def down_x(index, part, parts):
        return down.at[rest, :, lanes(index * parts + part, down_cols // parts)]

    rings = {
        "ux": (nx, x, x_peer, up_x, S_RING),
        "dy": (ny, y, y_peer, down_y, S_RING + 4),
        "uy": (ny, y, y_peer, up_y, S_RING + 8),
        "dx": (nx, x, x_peer, down_x, S_RING + 12),
    }

    def ring_start(name):
        n, at, peer, block, slot = rings[name]
        for k in sorted({1, n - 1} - {0}):
            own = block(at, 0, 1)
            remote(own, own, slot + (k != 1), peer(k)).start()

    def ring_turn(name):
        n, at, peer, block, slot = rings[name]
        if n > 1:
            wait_recv(block(at, 0, 1), slot)
        if n == 4:
            left = block(lax.rem(at + 3, 4), 0, 2)
            remote(left, left, slot + 2, peer(1)).start()
            wait_recv(block(at, 0, 1), slot + 1)
            right = block(lax.rem(at + 1, 4), 1, 2)
            remote(right, right, slot + 3, peer(3)).start()

    def ring_end(name):
        n, at, peer, block, slot = rings[name]
        if n == 4:
            wait_recv(block(at, 0, 2), slot + 2)
            wait_recv(block(at, 0, 2), slot + 3)

    def ring_sent(name):
        n, at, peer, block, slot = rings[name]
        for k in sorted({1, n - 1} - {0}):
            wait_send(block(at, 0, 1), slot + (k != 1))
        if n == 4:
            wait_send(block(at, 0, 2), slot + 2)
            wait_send(block(at, 0, 2), slot + 3)

    wait_recv(up.at[rest, up_piece, :], S_UP1)
    wait_recv(down.at[rest, down_piece[0], down_piece[1]], S_DOWN1)
    ring_start("ux")
    ring_start("dy")

    others = lat_rv.at[0].reshape(ng * 64, PAIR).at[pl.ds(0, (ng - 1) * 64), :]
    wait_recv(others, S_PROJ)
    remote(lat_rv.at[c], lat_rv.at[c], S_PROJ2, partner).start()
    ring_turn("ux")
    ring_turn("dy")

    wait_recv(lat_rv.at[other], S_PROJ2)
    lat_count = ng * 64
    lane = lax.broadcasted_iota(jnp.int32, (lat_count, PAIR), 1)
    keys = lat_rv[0].reshape(lat_count, PAIR).astype(F32) * HEAD_DIM ** (-0.5)
    values = lat_rv[1].reshape(lat_count, PAIR).astype(F32)
    for h in range(2):
        mine = (lane < HEAD_DIM) if h == 0 else (lane >= HEAD_DIM)
        km[h] = jnp.where(mine, keys, 0.0).astype(BF16)
        vm[h] = jnp.where(mine, values, 0.0).astype(BF16)

    ring_end("ux")
    ring_end("dy")
    ring_start("uy")
    ring_start("dx")

    cmax[...] = jnp.full(cmax.shape, -jnp.inf, F32)
    pair_lanes = lanes(z)

    def place(i):
        half = lax.div(i + 1, 2)
        return jnp.where(lax.rem(i, 2) == 1, half, lax.rem(nz - half, nz))

    def score_block(i):
        k = place(i)
        wait_recv(rv.at[0, k], S_REF + k)
        query = rv[0, k]
        for h in range(2):
            score = lax.dot_general(query, km[h], (((1,), (1,)), ((), ())), preferred_element_type=F32)
            scores[h, k] = score
            cmax[h] = jnp.maximum(cmax[h], jnp.max(score.reshape(rows // 8, 8, lat_count), axis=0))

    each(0, nz, score_block)

    peaks = [jnp.max(cmax[h], axis=0, keepdims=True) for h in range(2)]
    acc[...] = jnp.zeros(acc.shape, F32)
    wait_recv(rv.at[1], S_VAL)

    def columns(t):
        pair = rv[1, pl.ds(2 * t, 2)].reshape(2 * rows, PAIR)
        turned = pair.astype(F32).T.astype(BF16)
        ones = jnp.ones((16, 2 * rows), BF16)
        for h in range(2):
            score = scores[h, pl.ds(2 * t, 2)].reshape(2 * rows, lat_count)
            exponent = jnp.exp(score - peaks[h]).astype(BF16)
            left = jnp.concatenate([turned[h * HEAD_DIM : (h + 1) * HEAD_DIM], ones], axis=0)
            acc[h] = acc[h] + dot(left, exponent)

    each(0, nz // 2, columns)
    for h in range(2):
        acc[h, 72:80, :] = jnp.broadcast_to(peaks[h], (8, lat_count))
    remote(acc.at[other], col_in, S_COL, partner).start()

    def attend(i):
        k = place(nz - 1 - i)
        result = jnp.zeros((rows, PAIR), F32)
        for h in range(2):
            score = scores[h, k]
            exponent = jnp.exp(score - jnp.max(score, axis=1, keepdims=True))
            inverse = 1.0 / jnp.sum(exponent, axis=1, keepdims=True)
            result = result + dot((exponent * inverse).astype(BF16), vm[h])
        att_out[k] = result.astype(BF16)

        @pl.when(k == 0)
        def _():
            local(att_out.at[0], att.at[:, pair_lanes], S_ATT).start()

        @pl.when(k > 0)
        def _():
            device = (g, lax.rem(z + k, nz) * 2 + c)
            remote(att_out.at[k], att.at[:, pair_lanes], S_ATT, device).start()

    each(0, nz // 4, attend)

    wait_recv(col_in, S_COL)
    own_peak = acc[c, 72:80, :]
    in_peak = col_in[72:80, :]
    peak = jnp.maximum(own_peak, in_peak)
    own_scale = jnp.exp(own_peak - peak)
    in_scale = jnp.exp(in_peak - peak)
    own_sums = acc[c, 0:72, :].reshape(9, 8, lat_count)
    in_sums = col_in[0:72, :].reshape(9, 8, lat_count)
    sums = (own_sums * own_scale[None] + in_sums * in_scale[None]).reshape(72, lat_count)
    for b in range(ng):
        span = slice((b // 2) * PAIR, (b // 2 + 1) * PAIR)
        blk[b, 0:32, :] = sums[(b % 2) * 32 : (b % 2) * 32 + 32, span]
        blk[b, 32:36, :] = sums[64:68, span]
        blk[b, 36:40, :] = peak[0:4, span]

    def block_of(gg):
        return 2 * lax.rem(z + lax.div(gg, 2), nz) + lax.rem(gg, 2)

    def send_blk(k):
        gg = lax.rem(g + k, ng)
        remote(blk.at[block_of(gg)], rs.at[g], S_RS, (gg, m)).start()

    local(blk.at[block_of(g)], rs.at[g], S_RS).start()
    each(1, ng, send_blk)

    each(nz // 4, nz, attend)

    wait_recv(rs, S_RS)
    all_peaks = rs[:, 36:37, :]
    factor = jnp.exp(all_peaks - jnp.max(all_peaks, axis=0, keepdims=True))
    total = jnp.sum(rs[:, 32:33, :] * factor, axis=0)
    summed = jnp.sum(rs[:, 0:32, :] * factor, axis=0)
    zb[...] = summed / total

    @pl.when(owner == z)
    def _():
        local(zb, lab.at[g], S_ZC).start()

    @pl.when(owner != z)
    def _():
        remote(zb, lab.at[g], S_ZC, (g, owner * 2 + c)).start()

    ring_turn("uy")
    ring_turn("dx")
    wait_recv(att, S_ATT)
    loads[2].wait()
    mid[...] = tokens[...].astype(F32) + dot(att[...], wtok[2])
    mid32 = mid[...]
    mlp_in[c] = (mid32 * scale_of(mid32) * mlp_gain[...]).astype(BF16)
    remote(mlp_in.at[c], mlp_in.at[c], S_MIN, partner).start()

    wait_recv(zb, S_ZC)

    def send_lab(k):
        remote(lab.at[g], lab.at[g], S_AG, (lax.rem(g + k, ng), m)).start()

    each(1, ng, send_lab)

    loads[3].wait()
    loads[4].wait()
    wait_recv(mlp_in.at[other], S_MIN)
    ring_end("uy")
    both = mlp_in[...].reshape(2 * rows, width)
    for n in range(nz // 2):
        piece = jnp.concatenate([up[2 * n], up[2 * n + 1]], axis=1)
        hid[:, n * 256 : (n + 1) * 256] = gelu(dot(both, piece)).astype(BF16)

    wait_recv(lab.at[pl.ds(0, ng - 1)], S_AG)
    attended = lab[...].reshape(ng * 32, PAIR)
    sq[...] = jnp.broadcast_to(jnp.sum(attended * attended, axis=0, keepdims=True), (8, PAIR))
    remote(sq, sq_in, S_SQ, partner).start()

    ring_end("dx")
    half_width = width // 2
    step = min(256, half_width)

    def mlp_out(first, last, slot):
        for n in range(first, last, step):
            span = slice(n, n + step)
            made = dot(hid[...], down[:, :, span].reshape(hid.shape[1], step))
            mp[:, :, span] = made.reshape(2, rows, step)
        span = pl.ds(first, last - first)
        remote(mp.at[other, :, span], mp_in.at[:, span], slot, partner).start()

    mlp_out(0, half_width, S_MP0)

    wait_recv(sq_in, S_SQ)
    norm = lax.rsqrt((sq[0:1, :] + sq_in[0:1, :]) * (1.0 / width) + NORM_EPS)
    mixed = (attended * norm).T.astype(BF16)
    wait_recv(wout, S_WOUT)
    part[...] = dot(mixed, wout[...]).reshape(2, 64, PAIR)
    remote(part.at[other], part_in, S_PART, partner).start()

    mlp_out(half_width, width, S_MP1)

    wait_recv(part_in, S_PART)
    own_lanes = lanes(gpair)
    latents_out[:, own_lanes] = (
        latents[:, own_lanes].astype(F32) + (part[c] + part_in[...])
    ).astype(BF16)

    def send_lo(k):
        device = (2 * lax.rem(gpair + k, nz) + lax.rem(g, 2), m)
        remote(latents_out.at[:, own_lanes], latents_out.at[:, own_lanes], S_LO, device).start()

    each(1, nz, send_lo)

    for first, slot in ((0, S_MP0), (half_width, S_MP1)):
        span = slice(first, first + half_width)
        wait_recv(mp_in.at[:, pl.ds(first, half_width)], slot)
        tokens_out[:, span] = (mid[:, span] + (mp[c, :, span] + mp_in[:, span])).astype(BF16)

    wait_recv(latents_out.at[:, pl.ds(0, (nz - 1) * PAIR)], S_LO)

    @pl.when(y != 0)
    def _():
        wait_send(latx.at[0, 0], S_LAT)

    for _ in range(2 * high - 1):
        wait_send(latx.at[0, 0], S_LAT)

    @pl.when(owner != z)
    def _():
        wait_send(zb, S_ZC)

    wait_send(lab.at[pl.ds(0, ng - 1)], S_AG)
    wait_send(wlat.at[pl.ds(0, nm - 1), 0], S_W)
    wait_send(wlat.at[:, pl.ds(0, nx - 1)], S_W2)
    wait_send(up.at[rest, up_piece, :], S_UP1)
    wait_send(down.at[rest, down_piece[0], down_piece[1]], S_DOWN1)
    wait_send(rv.at[0, rest], S_REF)
    wait_send(rv.at[1, rest], S_VAL)
    wait_send(wout.at[pl.ds(0, (nz - 1) * 64), :], S_WOUT)
    wait_send(others, S_PROJ)
    wait_send(lat_rv.at[0], S_PROJ2)
    for name in rings:
        ring_sent(name)
    wait_send(att_out.at[pl.ds(1, nz - 1)], S_ATT)
    wait_send(col_in, S_COL)
    wait_send(mlp_in.at[0], S_MIN)
    wait_send(rs.at[pl.ds(0, ng - 1)], S_RS)
    wait_send(sq_in, S_SQ)
    wait_send(part_in, S_PART)
    wait_send(mp_in.at[:, pl.ds(0, half_width)], S_MP0)
    wait_send(mp_in.at[:, pl.ds(half_width, half_width)], S_MP1)
    wait_send(latents_out.at[:, pl.ds(0, (nz - 1) * PAIR)], S_LO)


def per_device(nx, ny, nz, *args):
    (tokens, latents, tok_gain, lat_gain, mlp_gain, *weights) = args
    ng = nx * ny
    rows, width = tokens.shape
    lat_count = latents.shape[0] * 2 * nz
    unit = weights[6].shape[1]
    vmem = pl.BlockSpec(memory_space=pltpu.VMEM)
    anywhere = pl.BlockSpec(memory_space=pl.ANY)
    scratch = [
        ((3, width, width), BF16),
        ((nz, width, unit), BF16),
        ((nz, unit, width), BF16),
        ((2 * nz, nx, 64 // nx, PAIR), BF16),
        ((nz // ny, 2, 64 // nx, width), BF16),
        ((nz * 64, PAIR), BF16),
        ((2, nz, rows, PAIR), BF16),
        ((2, nz, rows, PAIR), BF16),
        ((2, nz // ny, ny, 2, nx, 64 // nx, PAIR), BF16),
        ((2, lat_count, PAIR), BF16),
        ((2, lat_count, PAIR), BF16),
        ((2, nz, rows, lat_count), F32),
        ((2, 8, lat_count), F32),
        ((2, 80, lat_count), F32),
        ((nz, rows, PAIR), BF16),
        ((rows, width), BF16),
        ((80, lat_count), F32),
        ((ng, 40, PAIR), F32),
        ((ng, 40, PAIR), F32),
        ((32, PAIR), F32),
        ((ng, 32, PAIR), F32),
        ((8, PAIR), F32),
        ((8, PAIR), F32),
        ((2, 64, PAIR), F32),
        ((64, PAIR), F32),
        ((rows, width), F32),
        ((2, rows, width), BF16),
        ((2 * rows, nz * unit), BF16),
        ((2, rows, width), F32),
        ((rows, width), F32),
    ]
    return pl.pallas_call(
        functools.partial(kernel, nx, ny, nz),
        out_shape=(
            jax.ShapeDtypeStruct(tokens.shape, BF16),
            jax.ShapeDtypeStruct(latents.shape, BF16),
        ),
        in_specs=[vmem] * 5 + [anywhere] * 8,
        out_specs=(vmem, vmem),
        scratch_shapes=[pltpu.VMEM(shape, kind) for shape, kind in scratch]
        + [
            pltpu.SemaphoreType.DMA((5,)),
            pltpu.SemaphoreType.DMA((S_REF + 1,)),
            pltpu.SemaphoreType.DMA((S_REF + nz,)),
        ],
        compiler_params=pltpu.CompilerParams(
            collective_id=0, has_side_effects=True, vmem_limit_bytes=56 * 1024 * 1024
        ),
        name="layer",
    )(
        tokens,
        latents,
        tok_gain.reshape(1, width),
        lat_gain.reshape(1, width),
        mlp_gain.reshape(1, width),
        *weights,
    )


def solution(mesh):
    ng = mesh.shape["group"]
    nz = mesh.shape["member"] // 2
    nx = int(round(ng**0.5))
    in_specs = (
        P(("group", "member"), None),
        P("member", None),
        P(),
        P(),
        P(),
        P(),
        P(),
        P(),
        P("member", None),
        P("member", None),
        P("member", None),
        P(None, "member"),
        P("member", None),
    )
    out_specs = (P(("group", "member"), None), P("member", None))
    return jax.shard_map(
        functools.partial(per_device, nx, ng // nx, nz),
        mesh=mesh, in_specs=in_specs, out_specs=out_specs, check_vma=False,
    )
```

```python
import functools

import jax
import jax.numpy as jnp
from jax import lax
from jax.experimental import pallas as pl
from jax.experimental.pallas import tpu as pltpu
from jax.sharding import PartitionSpec as P

HEAD_DIM = 64
PAIR = 2 * HEAD_DIM
NORM_EPS = 1e-06
MESH = pl.DeviceIdType.MESH
F32 = jnp.float32
BF16 = jnp.bfloat16

(
    S_W, S_W2, S_LAT, S_UP1, S_DOWN1, S_WOUT, S_VAL, S_PROJ, S_PROJ2, S_ATT, S_COL, S_RS, S_ZC, S_AG,
    S_SQ, S_PART, S_LO, S_MIN, S_MP0, S_MP1,
) = range(20)
S_RING = 20
S_REF = 36


def scale_of(values):
    return lax.rsqrt(jnp.mean(values * values, axis=-1, keepdims=True) + NORM_EPS)


def dot(left_side, right_side):
    return jnp.dot(left_side, right_side, preferred_element_type=F32)


def gelu(values):
    return 0.5 * values * (1.0 + lax.erf(values * (0.5**0.5)))


def kernel(
    nx, ny, nz,
    tokens, latents, tok_gain, lat_gain, mlp_gain,
    w_ref_tok, w_val_tok, w_out_tok, w_ref_lat, w_val_lat, w_out_lat, w_up, w_down,
    tokens_out, latents_out,
    wtok, up, down, wlat, latx, wout, rvo, rv, lat_rv, km, vm, scores, cmax, acc, att_out, att,
    col_in, blk, rs, zb, lab, sq, sq_in, part, part_in, mid, mlp_in, hid, mp, mp_in,
    load, send, recv,
):
    ng = nx * ny
    nm = 2 * nz
    rows, width = tokens.shape
    g = lax.axis_index("group")
    m = lax.axis_index("member")
    z = lax.div(m, 2)
    c = lax.rem(m, 2)
    y = lax.div(g, nx)
    x = lax.rem(g, nx)
    other = 1 - c
    partner = (g, z * 2 + other)
    gpair = lax.div(g, 2)

    def remote(src, dst, slot, device):
        return pltpu.make_async_remote_copy(
            src_ref=src, dst_ref=dst, send_sem=send.at[min(slot, S_REF)] if isinstance(slot, int) else send.at[S_REF],
            recv_sem=recv.at[slot], device_id=device, device_id_type=MESH,
        )

    def local(src, dst, slot):
        return pltpu.make_async_copy(src, dst, recv.at[slot])

    def wait_recv(ref, slot):
        pltpu.make_async_copy(ref, ref, recv.at[slot]).wait()

    def wait_send(ref, slot):
        pltpu.make_async_copy(ref, ref, send.at[slot]).wait()

    def each(low, high, body):
        def step(i, carry):
            body(i)
            return carry

        lax.fori_loop(low, high, step, 0)

    def lanes(index, size=PAIR):
        return pl.ds(pl.multiple_of(index * size, size), size)

    def block_rows(index, size=64):
        return pl.ds(pl.multiple_of(index * size, size), size)

    loads = [
        pltpu.make_async_copy(w_ref_tok, wtok.at[0], load.at[0]),
        pltpu.make_async_copy(w_val_tok, wtok.at[1], load.at[1]),
        pltpu.make_async_copy(w_out_tok, wtok.at[2], load.at[2]),
        pltpu.make_async_copy(w_up, up.at[0], load.at[3]),
        pltpu.make_async_copy(w_down, down.at[0], load.at[4]),
    ]
    for item in loads:
        item.start()

    barrier = pltpu.get_barrier_semaphore()

    def greet(device):
        pl.semaphore_signal(barrier, inc=1, device_id=device, device_id_type=MESH)

    owner = lax.rem(z + gpair, nz)

    each(1, nm, lambda k: greet((g, lax.rem(m + k, nm))))
    each(1, ng, lambda k: greet((lax.rem(g + k, ng), m)))
    tok32 = tokens[...].astype(F32)
    tok_norm = (tok32 * scale_of(tok32) * tok_gain[...]).astype(BF16)

    def project_tokens(kind):
        for n in range(nz // 2):
            made = dot(tok_norm, wtok[kind, :, n * 256 : (n + 1) * 256]).astype(BF16)
            for i in range(2):
                rvo[kind, 2 * n + i] = made[:, i * PAIR : (i + 1) * PAIR]

    loads[0].wait()
    project_tokens(0)
    pl.semaphore_wait(barrier, nm + ng - 2)

    piece_rows = 64 // nx
    x_rows = block_rows(x, piece_rows)

    def send_w(k):
        zz = lax.rem(z + k, nz)
        remote(w_ref_lat.at[x_rows, lanes(zz)], wlat.at[m, x], S_W, (g, zz * 2)).start()
        remote(w_val_lat.at[x_rows, lanes(zz)], wlat.at[m, x], S_W, (g, zz * 2 + 1)).start()

    each(1, nz, send_w)

    @pl.when(c == 0)
    def _():
        local(w_ref_lat.at[x_rows, lanes(z)], wlat.at[m, x], S_W).start()
        remote(w_val_lat.at[x_rows, lanes(z)], wlat.at[m, x], S_W, partner).start()

    @pl.when(c == 1)
    def _():
        local(w_val_lat.at[x_rows, lanes(z)], wlat.at[m, x], S_W).start()
        remote(w_ref_lat.at[x_rows, lanes(z)], wlat.at[m, x], S_W, partner).start()

    high = nz // ny
    z_low = lax.rem(z, ny)
    z_high = lax.div(z, ny)
    for hh in range(high):
        zz = lax.rem(z_low + ny - y, ny) + ny * hh
        for cc in range(2):
            to_self = (zz == z) & (c == cc)

            @pl.when(to_self)
            def _():
                local(latents.at[x_rows, :], latx.at[z_high, c], S_LAT).start()

            @pl.when(jnp.logical_not(to_self))
            def _(zz=zz, cc=cc):
                remote(latents.at[x_rows, :], latx.at[z_high, c], S_LAT, (g, zz * 2 + cc)).start()

    up_rows = width // ng
    down_rows = down.shape[1] // ny
    down_cols = width // nx
    up_piece = block_rows(g, up_rows)
    down_piece = (block_rows(y, down_rows), lanes(x, down_cols))

    def send_mlp(k):
        device = (g, lax.rem(z + k, nz) * 2 + c)
        remote(w_up.at[up_piece, :], up.at[nz - k, up_piece, :], S_UP1, device).start()
        remote(
            w_down.at[down_piece[0], down_piece[1]],
            down.at[nz - k, down_piece[0], down_piece[1]], S_DOWN1, device,
        ).start()

    each(1, nz, send_mlp)
    local(rvo.at[0, z], rv.at[0, 0], S_REF).start()

    def send_ref(k):
        zz = lax.rem(z + k, nz)
        remote(rvo.at[0, zz], rv.at[0, nz - k], S_REF + nz - k, (g, zz * 2 + c)).start()

    each(1, nz, send_ref)

    def x_peer(k):
        return (y * nx + lax.rem(x + k, nx), m)

    def y_peer(k):
        return (lax.rem(y + k, ny) * nx + x, m)

    wait_recv(wlat.at[:, x], S_W)
    each(1, nx, lambda k: remote(wlat.at[:, x], wlat.at[:, x], S_W2, x_peer(k)).start())

    loads[1].wait()
    project_tokens(1)
    local(rvo.at[1, z], rv.at[1, 0], S_VAL).start()

    def send_val(k):
        zz = lax.rem(z + k, nz)
        remote(rvo.at[1, zz], rv.at[1, nz - k], S_VAL, (g, zz * 2 + c)).start()

    each(1, nz, send_val)

    def send_wout(k):
        device = (g, lax.rem(z + k, nz) * 2 + c)
        remote(w_out_lat.at[:, lanes(gpair)], wout.at[block_rows(k), :], S_WOUT, device).start()

    wait_recv(latx, S_LAT)
    lat32 = latx[...].reshape(64, width).astype(F32)
    lat_norm = (lat32 * scale_of(lat32) * lat_gain[...]).astype(BF16)
    wait_recv(wlat.at[:, pl.ds(0, nx - 1)], S_W2)
    made = dot(lat_norm, wlat[...].reshape(width, PAIR)).astype(BF16).reshape(high, 2, piece_rows, PAIR)
    low = lax.rem(z + y, ny)
    for hh in range(high):
        for cc in range(2):
            lat_rv[c, hh, low, cc, x] = made[hh, cc]

    def send_proj(k):
        block = lat_rv.at[c, :, low, :, x]
        remote(block, block, S_PROJ, (lax.rem(g + k, ng), m)).start()

    each(1, ng, send_proj)

    local(w_out_lat.at[:, lanes(gpair)], wout.at[pl.ds(0, 64), :], S_WOUT).start()
    each(1, nz, send_wout)

    rest = pl.ds(1, nz - 1)

    def up_x(index, part, parts):
        size = up_rows // parts
        return up.at[rest, block_rows((y * nx + index) * parts + part, size), :]

    def up_y(index, part, parts):
        size = nx * up_rows // parts
        return up.at[rest, block_rows(index * parts + part, size), :]

    def down_y(index, part, parts):
        size = down_rows // parts
        return down.at[rest, block_rows(index * parts + part, size), lanes(x, down_cols)]

    def down_x(index, part, parts):
        return down.at[rest, :, lanes(index * parts + part, down_cols // parts)]

    rings = {
        "ux": (nx, x, x_peer, up_x, S_RING),
        "dy": (ny, y, y_peer, down_y, S_RING + 4),
        "uy": (ny, y, y_peer, up_y, S_RING + 8),
        "dx": (nx, x, x_peer, down_x, S_RING + 12),
    }

    def ring_start(name):
        n, at, peer, block, slot = rings[name]
        for k in sorted({1, n - 1} - {0}):
            own = block(at, 0, 1)
            remote(own, own, slot + (k != 1), peer(k)).start()

    def ring_turn(name):
        n, at, peer, block, slot = rings[name]
        if n > 1:
            wait_recv(block(at, 0, 1), slot)
        if n == 4:
            left = block(lax.rem(at + 3, 4), 0, 2)
            remote(left, left, slot + 2, peer(1)).start()
            wait_recv(block(at, 0, 1), slot + 1)
            right = block(lax.rem(at + 1, 4), 1, 2)
            remote(right, right, slot + 3, peer(3)).start()

    def ring_end(name):
        n, at, peer, block, slot = rings[name]
        if n == 4:
            wait_recv(block(at, 0, 2), slot + 2)
            wait_recv(block(at, 0, 2), slot + 3)

    def ring_sent(name):
        n, at, peer, block, slot = rings[name]
        for k in sorted({1, n - 1} - {0}):
            wait_send(block(at, 0, 1), slot + (k != 1))
        if n == 4:
            wait_send(block(at, 0, 2), slot + 2)
            wait_send(block(at, 0, 2), slot + 3)

    wait_recv(up.at[rest, up_piece, :], S_UP1)
    wait_recv(down.at[rest, down_piece[0], down_piece[1]], S_DOWN1)
    ring_start("ux")
    ring_start("dy")

    others = lat_rv.at[0].reshape(ng * 64, PAIR).at[pl.ds(0, (ng - 1) * 64), :]
    wait_recv(others, S_PROJ)
    remote(lat_rv.at[c], lat_rv.at[c], S_PROJ2, partner).start()
    ring_turn("ux")
    ring_turn("dy")

    wait_recv(lat_rv.at[other], S_PROJ2)
    lat_count = ng * 64
    lane = lax.broadcasted_iota(jnp.int32, (lat_count, PAIR), 1)

    def keep_head(array, h):
        mine = (lane < HEAD_DIM) if h == 0 else (lane >= HEAD_DIM)
        return jnp.where(mine, array, 0.0).astype(BF16)

    keys = lat_rv[0].reshape(lat_count, PAIR).astype(F32) * HEAD_DIM ** (-0.5)
    for h in range(2):
        km[h] = keep_head(keys, h)

    ring_end("ux")
    ring_end("dy")
    ring_start("uy")
    ring_start("dx")

    cmax[...] = jnp.full(cmax.shape, -jnp.inf, F32)
    pair_lanes = lanes(z)

    def place(i):
        half = lax.div(i + 1, 2)
        return jnp.where(lax.rem(i, 2) == 1, half, lax.rem(nz - half, nz))

    def score_block(i):
        k = place(i)
        wait_recv(rv.at[0, k], S_REF + k)
        query = rv[0, k]
        for h in range(2):
            score = lax.dot_general(query, km[h], (((1,), (1,)), ((), ())), preferred_element_type=F32)
            scores[h, k] = score
            cmax[h] = jnp.maximum(cmax[h], jnp.max(score.reshape(rows // 8, 8, lat_count), axis=0))

    each(0, nz, score_block)

    peaks = [jnp.max(cmax[h], axis=0, keepdims=True) for h in range(2)]
    acc[...] = jnp.zeros(acc.shape, F32)
    wait_recv(rv.at[1], S_VAL)

    def columns(t):
        pair = rv[1, pl.ds(2 * t, 2)].reshape(2 * rows, PAIR)
        turned = pair.astype(F32).T.astype(BF16)
        ones = jnp.ones((16, 2 * rows), BF16)
        for h in range(2):
            score = scores[h, pl.ds(2 * t, 2)].reshape(2 * rows, lat_count)
            exponent = jnp.exp(score - peaks[h]).astype(BF16)
            left = jnp.concatenate([turned[h * HEAD_DIM : (h + 1) * HEAD_DIM], ones], axis=0)
            acc[h] = acc[h] + dot(left, exponent)

    each(0, nz // 2, columns)
    for h in range(2):
        acc[h, 72:80, :] = jnp.broadcast_to(peaks[h], (8, lat_count))
    remote(acc.at[other], col_in, S_COL, partner).start()

    values = lat_rv[1].reshape(lat_count, PAIR).astype(F32)
    for h in range(2):
        vm[h] = keep_head(values, h)

    def attend(i):
        k = place(nz - 1 - i)
        result = jnp.zeros((rows, PAIR), F32)
        for h in range(2):
            score = scores[h, k]
            exponent = jnp.exp(score - jnp.max(score, axis=1, keepdims=True))
            inverse = 1.0 / jnp.sum(exponent, axis=1, keepdims=True)
            result = result + dot((exponent * inverse).astype(BF16), vm[h])
        att_out[k] = result.astype(BF16)

        @pl.when(k == 0)
        def _():
            local(att_out.at[0], att.at[:, pair_lanes], S_ATT).start()

        @pl.when(k > 0)
        def _():
            device = (g, lax.rem(z + k, nz) * 2 + c)
            remote(att_out.at[k], att.at[:, pair_lanes], S_ATT, device).start()

    each(0, nz // 4, attend)

    wait_recv(col_in, S_COL)
    own_peak = acc[c, 72:80, :]
    in_peak = col_in[72:80, :]
    peak = jnp.maximum(own_peak, in_peak)
    own_scale = jnp.exp(own_peak - peak)
    in_scale = jnp.exp(in_peak - peak)
    own_sums = acc[c, 0:72, :].reshape(9, 8, lat_count)
    in_sums = col_in[0:72, :].reshape(9, 8, lat_count)
    sums = (own_sums * own_scale[None] + in_sums * in_scale[None]).reshape(72, lat_count)
    for b in range(ng):
        span = slice((b // 2) * PAIR, (b // 2 + 1) * PAIR)
        blk[b, 0:32, :] = sums[(b % 2) * 32 : (b % 2) * 32 + 32, span]
        blk[b, 32:36, :] = sums[64:68, span]
        blk[b, 36:40, :] = peak[0:4, span]

    def block_of(gg):
        return 2 * lax.rem(z + lax.div(gg, 2), nz) + lax.rem(gg, 2)

    def send_blk(k):
        gg = lax.rem(g + k, ng)
        remote(blk.at[block_of(gg)], rs.at[g], S_RS, (gg, m)).start()

    local(blk.at[block_of(g)], rs.at[g], S_RS).start()
    each(1, ng, send_blk)

    each(nz // 4, nz, attend)

    wait_recv(rs, S_RS)
    all_peaks = rs[:, 36:37, :]
    factor = jnp.exp(all_peaks - jnp.max(all_peaks, axis=0, keepdims=True))
    total = jnp.sum(rs[:, 32:33, :] * factor, axis=0)
    summed = jnp.sum(rs[:, 0:32, :] * factor, axis=0)
    zb[...] = summed / total

    @pl.when(owner == z)
    def _():
        local(zb, lab.at[g], S_ZC).start()

    @pl.when(owner != z)
    def _():
        remote(zb, lab.at[g], S_ZC, (g, owner * 2 + c)).start()

    ring_turn("uy")
    ring_turn("dx")
    wait_recv(zb, S_ZC)

    def send_lab(k):
        remote(lab.at[g], lab.at[g], S_AG, (lax.rem(g + k, ng), m)).start()

    each(1, ng, send_lab)

    wait_recv(att, S_ATT)
    loads[2].wait()
    mid[...] = tokens[...].astype(F32) + dot(att[...], wtok[2])
    mid32 = mid[...]
    mlp_in[c] = (mid32 * scale_of(mid32) * mlp_gain[...]).astype(BF16)
    remote(mlp_in.at[c], mlp_in.at[c], S_MIN, partner).start()

    loads[3].wait()
    loads[4].wait()
    wait_recv(mlp_in.at[other], S_MIN)
    ring_end("uy")
    both = mlp_in[...].reshape(2 * rows, width)
    for n in range(nz // 2):
        piece = jnp.concatenate([up[2 * n], up[2 * n + 1]], axis=1)
        hid[:, n * 256 : (n + 1) * 256] = gelu(dot(both, piece)).astype(BF16)

    wait_recv(lab.at[pl.ds(0, ng - 1)], S_AG)
    attended = lab[...].reshape(ng * 32, PAIR)
    sq[...] = jnp.broadcast_to(jnp.sum(attended * attended, axis=0, keepdims=True), (8, PAIR))
    remote(sq, sq_in, S_SQ, partner).start()

    ring_end("dx")
    half_width = width // 2
    step = min(256, half_width)

    def mlp_out(first, last, slot):
        for n in range(first, last, step):
            span = slice(n, n + step)
            made = dot(hid[...], down[:, :, span].reshape(hid.shape[1], step))
            mp[:, :, span] = made.reshape(2, rows, step)
        span = pl.ds(first, last - first)
        remote(mp.at[other, :, span], mp_in.at[:, span], slot, partner).start()

    mlp_out(0, half_width, S_MP0)

    wait_recv(sq_in, S_SQ)
    norm = lax.rsqrt((sq[0:1, :] + sq_in[0:1, :]) * (1.0 / width) + NORM_EPS)
    mixed = (attended * norm).T.astype(BF16)
    wait_recv(wout, S_WOUT)
    part[...] = dot(mixed, wout[...]).reshape(2, 64, PAIR)
    remote(part.at[other], part_in, S_PART, partner).start()

    mlp_out(half_width, width, S_MP1)

    wait_recv(part_in, S_PART)
    own_lanes = lanes(gpair)
    latents_out[:, own_lanes] = (
        latents[:, own_lanes].astype(F32) + (part[c] + part_in[...])
    ).astype(BF16)

    def send_lo(k):
        device = (2 * lax.rem(gpair + k, nz) + lax.rem(g, 2), m)
        remote(latents_out.at[:, own_lanes], latents_out.at[:, own_lanes], S_LO, device).start()

    each(1, nz, send_lo)

    for first, slot in ((0, S_MP0), (half_width, S_MP1)):
        span = slice(first, first + half_width)
        wait_recv(mp_in.at[:, pl.ds(first, half_width)], slot)
        tokens_out[:, span] = (mid[:, span] + (mp[c, :, span] + mp_in[:, span])).astype(BF16)

    wait_recv(latents_out.at[:, pl.ds(0, (nz - 1) * PAIR)], S_LO)

    @pl.when(y != 0)
    def _():
        wait_send(latx.at[0, 0], S_LAT)

    for _ in range(2 * high - 1):
        wait_send(latx.at[0, 0], S_LAT)

    @pl.when(owner != z)
    def _():
        wait_send(zb, S_ZC)

    wait_send(lab.at[pl.ds(0, ng - 1)], S_AG)
    wait_send(wlat.at[pl.ds(0, nm - 1), 0], S_W)
    wait_send(wlat.at[:, pl.ds(0, nx - 1)], S_W2)
    wait_send(up.at[rest, up_piece, :], S_UP1)
    wait_send(down.at[rest, down_piece[0], down_piece[1]], S_DOWN1)
    wait_send(rv.at[0, rest], S_REF)
    wait_send(rv.at[1, rest], S_VAL)
    wait_send(wout.at[pl.ds(0, (nz - 1) * 64), :], S_WOUT)
    wait_send(others, S_PROJ)
    wait_send(lat_rv.at[0], S_PROJ2)
    for name in rings:
        ring_sent(name)
    wait_send(att_out.at[pl.ds(1, nz - 1)], S_ATT)
    wait_send(col_in, S_COL)
    wait_send(mlp_in.at[0], S_MIN)
    wait_send(rs.at[pl.ds(0, ng - 1)], S_RS)
    wait_send(sq_in, S_SQ)
    wait_send(part_in, S_PART)
    wait_send(mp_in.at[:, pl.ds(0, half_width)], S_MP0)
    wait_send(mp_in.at[:, pl.ds(half_width, half_width)], S_MP1)
    wait_send(latents_out.at[:, pl.ds(0, (nz - 1) * PAIR)], S_LO)


def per_device(nx, ny, nz, *args):
    (tokens, latents, tok_gain, lat_gain, mlp_gain, *weights) = args
    ng = nx * ny
    rows, width = tokens.shape
    lat_count = latents.shape[0] * 2 * nz
    unit = weights[6].shape[1]
    vmem = pl.BlockSpec(memory_space=pltpu.VMEM)
    anywhere = pl.BlockSpec(memory_space=pl.ANY)
    scratch = [
        ((3, width, width), BF16),
        ((nz, width, unit), BF16),
        ((nz, unit, width), BF16),
        ((2 * nz, nx, 64 // nx, PAIR), BF16),
        ((nz // ny, 2, 64 // nx, width), BF16),
        ((nz * 64, PAIR), BF16),
        ((2, nz, rows, PAIR), BF16),
        ((2, nz, rows, PAIR), BF16),
        ((2, nz // ny, ny, 2, nx, 64 // nx, PAIR), BF16),
        ((2, lat_count, PAIR), BF16),
        ((2, lat_count, PAIR), BF16),
        ((2, nz, rows, lat_count), F32),
        ((2, 8, lat_count), F32),
        ((2, 80, lat_count), F32),
        ((nz, rows, PAIR), BF16),
        ((rows, width), BF16),
        ((80, lat_count), F32),
        ((ng, 40, PAIR), F32),
        ((ng, 40, PAIR), F32),
        ((32, PAIR), F32),
        ((ng, 32, PAIR), F32),
        ((8, PAIR), F32),
        ((8, PAIR), F32),
        ((2, 64, PAIR), F32),
        ((64, PAIR), F32),
        ((rows, width), F32),
        ((2, rows, width), BF16),
        ((2 * rows, nz * unit), BF16),
        ((2, rows, width), F32),
        ((rows, width), F32),
    ]
    return pl.pallas_call(
        functools.partial(kernel, nx, ny, nz),
        out_shape=(
            jax.ShapeDtypeStruct(tokens.shape, BF16),
            jax.ShapeDtypeStruct(latents.shape, BF16),
        ),
        in_specs=[vmem] * 5 + [anywhere] * 8,
        out_specs=(vmem, vmem),
        scratch_shapes=[pltpu.VMEM(shape, kind) for shape, kind in scratch]
        + [
            pltpu.SemaphoreType.DMA((5,)),
            pltpu.SemaphoreType.DMA((S_REF + 1,)),
            pltpu.SemaphoreType.DMA((S_REF + nz,)),
        ],
        compiler_params=pltpu.CompilerParams(
            collective_id=0, has_side_effects=True, vmem_limit_bytes=56 * 1024 * 1024
        ),
        name="layer",
    )(
        tokens,
        latents,
        tok_gain.reshape(1, width),
        lat_gain.reshape(1, width),
        mlp_gain.reshape(1, width),
        *weights,
    )


def solution(mesh):
    ng = mesh.shape["group"]
    nz = mesh.shape["member"] // 2
    nx = int(round(ng**0.5))
    in_specs = (
        P(("group", "member"), None),
        P("member", None),
        P(),
        P(),
        P(),
        P(),
        P(),
        P(),
        P("member", None),
        P("member", None),
        P("member", None),
        P(None, "member"),
        P("member", None),
    )
    out_specs = (P(("group", "member"), None), P("member", None))
    return jax.shard_map(
        functools.partial(per_device, nx, ng // nx, nz),
        mesh=mesh, in_specs=in_specs, out_specs=out_specs, check_vma=False,
    )
```

```python
import functools

import jax
import jax.numpy as jnp
from jax import lax
from jax.experimental import pallas as pl
from jax.experimental.pallas import tpu as pltpu
from jax.sharding import PartitionSpec as P

HEAD_DIM = 64
PAIR = 2 * HEAD_DIM
NORM_EPS = 1e-06
MESH = pl.DeviceIdType.MESH
F32 = jnp.float32
BF16 = jnp.bfloat16

(
    S_W, S_W2, S_LAT, S_UP1, S_DOWN1, S_WOUT, S_VAL, S_PROJ, S_PROJ2, S_ATT, S_COL, S_RS, S_ZC, S_AG,
    S_SQ, S_PART, S_LO, S_MIN, S_MP0, S_MP1,
) = range(20)
S_RING = 20
S_REF = 36


def scale_of(values):
    return lax.rsqrt(jnp.mean(values * values, axis=-1, keepdims=True) + NORM_EPS)


def dot(left_side, right_side):
    return jnp.dot(left_side, right_side, preferred_element_type=F32)


def gelu(values):
    return 0.5 * values * (1.0 + lax.erf(values * (0.5**0.5)))


def kernel(
    nx, ny, nz,
    tokens, latents, tok_gain, lat_gain, mlp_gain,
    w_ref_tok, w_val_tok, w_out_tok, w_ref_lat, w_val_lat, w_out_lat, w_up, w_down,
    tokens_out, latents_out,
    wtok, up, down, wlat, latx, wout, rvo, rv, lat_rv, km, vm, scores, cmax, acc, att_out, att,
    col_in, blk, rs, zb, lab, sq, sq_in, part, part_in, mid, mlp_in, hid, mp, mp_in,
    load, send, recv, heard,
):
    ng = nx * ny
    nm = 2 * nz
    rows, width = tokens.shape
    g = lax.axis_index("group")
    m = lax.axis_index("member")
    z = lax.div(m, 2)
    c = lax.rem(m, 2)
    y = lax.div(g, nx)
    x = lax.rem(g, nx)
    other = 1 - c
    partner = (g, z * 2 + other)
    gpair = lax.div(g, 2)

    def remote(src, dst, slot, device):
        return pltpu.make_async_remote_copy(
            src_ref=src, dst_ref=dst, send_sem=send.at[min(slot, S_REF)] if isinstance(slot, int) else send.at[S_REF],
            recv_sem=recv.at[slot], device_id=device, device_id_type=MESH,
        )

    def local(src, dst, slot):
        return pltpu.make_async_copy(src, dst, recv.at[slot])

    def wait_recv(ref, slot):
        pltpu.make_async_copy(ref, ref, recv.at[slot]).wait()

    def wait_send(ref, slot):
        pltpu.make_async_copy(ref, ref, send.at[slot]).wait()

    def each(low, high, body):
        def step(i, carry):
            body(i)
            return carry

        lax.fori_loop(low, high, step, 0)

    def lanes(index, size=PAIR):
        return pl.ds(pl.multiple_of(index * size, size), size)

    def block_rows(index, size=64):
        return pl.ds(pl.multiple_of(index * size, size), size)

    loads = [
        pltpu.make_async_copy(w_ref_tok, wtok.at[0], load.at[0]),
        pltpu.make_async_copy(w_val_tok, wtok.at[1], load.at[1]),
        pltpu.make_async_copy(w_out_tok, wtok.at[2], load.at[2]),
        pltpu.make_async_copy(w_up, up.at[0], load.at[3]),
        pltpu.make_async_copy(w_down, down.at[0], load.at[4]),
    ]
    for item in loads:
        item.start()

    def x_peer(k):
        return (y * nx + lax.rem(x + k, nx), m)

    def y_peer(k):
        return (lax.rem(y + k, ny) * nx + x, m)

    barrier = pltpu.get_barrier_semaphore()

    def greet(device):
        pl.semaphore_signal(barrier, inc=1, device_id=device, device_id_type=MESH)

    owner = lax.rem(z + gpair, nz)

    greet(partner)
    each(1, nz, lambda k: greet((g, lax.rem(z + k, nz) * 2 + c)))
    each(1, nx, lambda k: greet(x_peer(k)))
    each(1, ny, lambda k: greet(y_peer(k)))
    tok32 = tokens[...].astype(F32)
    tok_norm = (tok32 * scale_of(tok32) * tok_gain[...]).astype(BF16)

    def project_tokens(kind):
        for n in range(nz // 2):
            made = dot(tok_norm, wtok[kind, :, n * 256 : (n + 1) * 256]).astype(BF16)
            for i in range(2):
                rvo[kind, 2 * n + i] = made[:, i * PAIR : (i + 1) * PAIR]

    loads[0].wait()
    project_tokens(0)
    pl.semaphore_wait(barrier, nz + nx - 1 + ny - 1)

    def tell(sem, device):
        pl.semaphore_signal(sem, inc=1, device_id=device, device_id_type=MESH)

    tell(heard.at[0], partner)
    each(1, ny, lambda k: tell(heard.at[1], y_peer(k)))

    piece_rows = 64 // nx
    x_rows = block_rows(x, piece_rows)

    def send_w(core):
        source = w_val_lat if core else w_ref_lat

        def send_one(k):
            zz = lax.rem(z + k, nz)
            remote(source.at[x_rows, lanes(zz)], wlat.at[m, x], S_W, (g, zz * 2 + core)).start()

        each(1, nz, send_one)

    for core in range(2):

        @pl.when(c == core)
        def _(core=core):
            source, across = (w_val_lat, w_ref_lat) if core else (w_ref_lat, w_val_lat)
            local(source.at[x_rows, lanes(z)], wlat.at[m, x], S_W).start()
            send_w(core)
            remote(across.at[x_rows, lanes(z)], wlat.at[m, x], S_W, partner).start()
            pl.semaphore_wait(heard.at[0], 1)
            send_w(1 - core)

    high = nz // ny
    z_low = lax.rem(z, ny)
    z_high = lax.div(z, ny)
    for hh in range(high):
        zz = lax.rem(z_low + ny - y, ny) + ny * hh
        for cc in range(2):
            to_self = (zz == z) & (c == cc)

            @pl.when(to_self)
            def _():
                local(latents.at[x_rows, :], latx.at[z_high, c], S_LAT).start()

            @pl.when(jnp.logical_not(to_self))
            def _(zz=zz, cc=cc):
                remote(latents.at[x_rows, :], latx.at[z_high, c], S_LAT, (g, zz * 2 + cc)).start()

    up_rows = width // ng
    down_rows = down.shape[1] // ny
    down_cols = width // nx
    up_piece = block_rows(g, up_rows)
    down_piece = (block_rows(y, down_rows), lanes(x, down_cols))

    def send_mlp(k):
        device = (g, lax.rem(z + k, nz) * 2 + c)
        remote(w_up.at[up_piece, :], up.at[nz - k, up_piece, :], S_UP1, device).start()
        remote(
            w_down.at[down_piece[0], down_piece[1]],
            down.at[nz - k, down_piece[0], down_piece[1]], S_DOWN1, device,
        ).start()

    each(1, nz, send_mlp)
    local(rvo.at[0, z], rv.at[0, 0], S_REF).start()

    def send_ref(k):
        zz = lax.rem(z + k, nz)
        remote(rvo.at[0, zz], rv.at[0, nz - k], S_REF + nz - k, (g, zz * 2 + c)).start()

    each(1, nz, send_ref)

    wait_recv(wlat.at[:, x], S_W)
    each(1, nx, lambda k: remote(wlat.at[:, x], wlat.at[:, x], S_W2, x_peer(k)).start())

    loads[1].wait()
    project_tokens(1)
    local(rvo.at[1, z], rv.at[1, 0], S_VAL).start()

    def send_val(k):
        zz = lax.rem(z + k, nz)
        remote(rvo.at[1, zz], rv.at[1, nz - k], S_VAL, (g, zz * 2 + c)).start()

    each(1, nz, send_val)

    def send_wout(k):
        device = (g, lax.rem(z + k, nz) * 2 + c)
        remote(w_out_lat.at[:, lanes(gpair)], wout.at[block_rows(k), :], S_WOUT, device).start()

    wait_recv(latx, S_LAT)
    lat32 = latx[...].reshape(64, width).astype(F32)
    lat_norm = (lat32 * scale_of(lat32) * lat_gain[...]).astype(BF16)
    wait_recv(wlat.at[:, pl.ds(0, nx - 1)], S_W2)
    made = dot(lat_norm, wlat[...].reshape(width, PAIR)).astype(BF16).reshape(high, 2, piece_rows, PAIR)
    low = lax.rem(z + y, ny)
    for hh in range(high):
        for cc in range(2):
            lat_rv[c, hh, low, cc, x] = made[hh, cc]

    def send_proj(k):
        block = lat_rv.at[c, :, low, :, x]
        remote(block, block, S_PROJ, (lax.rem(g + k, ng), m)).start()

    pl.semaphore_wait(heard.at[1], ny - 1)
    each(1, ng, send_proj)

    local(w_out_lat.at[:, lanes(gpair)], wout.at[pl.ds(0, 64), :], S_WOUT).start()
    each(1, nz, send_wout)

    rest = pl.ds(1, nz - 1)

    def up_x(index, part, parts):
        size = up_rows // parts
        return up.at[rest, block_rows((y * nx + index) * parts + part, size), :]

    def up_y(index, part, parts):
        size = nx * up_rows // parts
        return up.at[rest, block_rows(index * parts + part, size), :]

    def down_y(index, part, parts):
        size = down_rows // parts
        return down.at[rest, block_rows(index * parts + part, size), lanes(x, down_cols)]

    def down_x(index, part, parts):
        return down.at[rest, :, lanes(index * parts + part, down_cols // parts)]

    rings = {
        "ux": (nx, x, x_peer, up_x, S_RING),
        "dy": (ny, y, y_peer, down_y, S_RING + 4),
        "uy": (ny, y, y_peer, up_y, S_RING + 8),
        "dx": (nx, x, x_peer, down_x, S_RING + 12),
    }

    def ring_start(name):
        n, at, peer, block, slot = rings[name]
        for k in sorted({1, n - 1} - {0}):
            own = block(at, 0, 1)
            remote(own, own, slot + (k != 1), peer(k)).start()

    def ring_turn(name):
        n, at, peer, block, slot = rings[name]
        if n > 1:
            wait_recv(block(at, 0, 1), slot)
        if n == 4:
            left = block(lax.rem(at + 3, 4), 0, 2)
            remote(left, left, slot + 2, peer(1)).start()
            wait_recv(block(at, 0, 1), slot + 1)
            right = block(lax.rem(at + 1, 4), 1, 2)
            remote(right, right, slot + 3, peer(3)).start()

    def ring_end(name):
        n, at, peer, block, slot = rings[name]
        if n == 4:
            wait_recv(block(at, 0, 2), slot + 2)
            wait_recv(block(at, 0, 2), slot + 3)

    def ring_sent(name):
        n, at, peer, block, slot = rings[name]
        for k in sorted({1, n - 1} - {0}):
            wait_send(block(at, 0, 1), slot + (k != 1))
        if n == 4:
            wait_send(block(at, 0, 2), slot + 2)
            wait_send(block(at, 0, 2), slot + 3)

    wait_recv(up.at[rest, up_piece, :], S_UP1)
    wait_recv(down.at[rest, down_piece[0], down_piece[1]], S_DOWN1)
    ring_start("ux")
    ring_start("dy")

    others = lat_rv.at[0].reshape(ng * 64, PAIR).at[pl.ds(0, (ng - 1) * 64), :]
    wait_recv(others, S_PROJ)
    remote(lat_rv.at[c], lat_rv.at[c], S_PROJ2, partner).start()
    ring_turn("ux")
    ring_turn("dy")

    wait_recv(lat_rv.at[other], S_PROJ2)
    lat_count = ng * 64
    lane = lax.broadcasted_iota(jnp.int32, (lat_count, PAIR), 1)

    def keep_head(array, h):
        mine = (lane < HEAD_DIM) if h == 0 else (lane >= HEAD_DIM)
        return jnp.where(mine, array, 0.0).astype(BF16)

    keys = lat_rv[0].reshape(lat_count, PAIR).astype(F32) * HEAD_DIM ** (-0.5)
    for h in range(2):
        km[h] = keep_head(keys, h)

    ring_end("ux")
    ring_end("dy")
    ring_start("uy")
    ring_start("dx")

    cmax[...] = jnp.full(cmax.shape, -jnp.inf, F32)
    pair_lanes = lanes(z)

    def place(i):
        half = lax.div(i + 1, 2)
        return jnp.where(lax.rem(i, 2) == 1, half, lax.rem(nz - half, nz))

    def score_block(i):
        k = place(i)
        wait_recv(rv.at[0, k], S_REF + k)
        query = rv[0, k]
        for h in range(2):
            score = lax.dot_general(query, km[h], (((1,), (1,)), ((), ())), preferred_element_type=F32)
            scores[h, k] = score
            cmax[h] = jnp.maximum(cmax[h], jnp.max(score.reshape(rows // 8, 8, lat_count), axis=0))

    each(0, nz, score_block)

    peaks = [jnp.max(cmax[h], axis=0, keepdims=True) for h in range(2)]
    acc[...] = jnp.zeros(acc.shape, F32)
    wait_recv(rv.at[1], S_VAL)

    def columns(t):
        pair = rv[1, pl.ds(2 * t, 2)].reshape(2 * rows, PAIR)
        turned = pair.astype(F32).T.astype(BF16)
        ones = jnp.ones((16, 2 * rows), BF16)
        for h in range(2):
            score = scores[h, pl.ds(2 * t, 2)].reshape(2 * rows, lat_count)
            exponent = jnp.exp(score - peaks[h]).astype(BF16)
            left = jnp.concatenate([turned[h * HEAD_DIM : (h + 1) * HEAD_DIM], ones], axis=0)
            acc[h] = acc[h] + dot(left, exponent)

    each(0, nz // 2, columns)
    for h in range(2):
        acc[h, 72:80, :] = jnp.broadcast_to(peaks[h], (8, lat_count))
    remote(acc.at[other], col_in, S_COL, partner).start()

    values = lat_rv[1].reshape(lat_count, PAIR).astype(F32)
    for h in range(2):
        vm[h] = keep_head(values, h)

    def attend(i):
        k = place(nz - 1 - i)
        result = jnp.zeros((rows, PAIR), F32)
        for h in range(2):
            score = scores[h, k]
            exponent = jnp.exp(score - jnp.max(score, axis=1, keepdims=True))
            inverse = 1.0 / jnp.sum(exponent, axis=1, keepdims=True)
            result = result + dot((exponent * inverse).astype(BF16), vm[h])
        att_out[k] = result.astype(BF16)

        @pl.when(k == 0)
        def _():
            local(att_out.at[0], att.at[:, pair_lanes], S_ATT).start()

        @pl.when(k > 0)
        def _():
            device = (g, lax.rem(z + k, nz) * 2 + c)
            remote(att_out.at[k], att.at[:, pair_lanes], S_ATT, device).start()

    each(0, nz // 4, attend)

    wait_recv(col_in, S_COL)
    own_peak = acc[c, 72:80, :]
    in_peak = col_in[72:80, :]
    peak = jnp.maximum(own_peak, in_peak)
    own_scale = jnp.exp(own_peak - peak)
    in_scale = jnp.exp(in_peak - peak)
    own_sums = acc[c, 0:72, :].reshape(9, 8, lat_count)
    in_sums = col_in[0:72, :].reshape(9, 8, lat_count)
    sums = (own_sums * own_scale[None] + in_sums * in_scale[None]).reshape(72, lat_count)
    for b in range(ng):
        span = slice((b // 2) * PAIR, (b // 2 + 1) * PAIR)
        blk[b, 0:32, :] = sums[(b % 2) * 32 : (b % 2) * 32 + 32, span]
        blk[b, 32:36, :] = sums[64:68, span]
        blk[b, 36:40, :] = peak[0:4, span]

    def block_of(gg):
        return 2 * lax.rem(z + lax.div(gg, 2), nz) + lax.rem(gg, 2)

    def send_blk(k):
        gg = lax.rem(g + k, ng)
        remote(blk.at[block_of(gg)], rs.at[g], S_RS, (gg, m)).start()

    local(blk.at[block_of(g)], rs.at[g], S_RS).start()
    each(1, ng, send_blk)

    each(nz // 4, nz, attend)

    wait_recv(rs, S_RS)
    all_peaks = rs[:, 36:37, :]
    factor = jnp.exp(all_peaks - jnp.max(all_peaks, axis=0, keepdims=True))
    total = jnp.sum(rs[:, 32:33, :] * factor, axis=0)
    summed = jnp.sum(rs[:, 0:32, :] * factor, axis=0)
    zb[...] = summed / total

    @pl.when(owner == z)
    def _():
        local(zb, lab.at[g], S_ZC).start()

    @pl.when(owner != z)
    def _():
        remote(zb, lab.at[g], S_ZC, (g, owner * 2 + c)).start()

    ring_turn("uy")
    ring_turn("dx")
    wait_recv(zb, S_ZC)

    def send_lab(k):
        remote(lab.at[g], lab.at[g], S_AG, (lax.rem(g + k, ng), m)).start()

    each(1, ng, send_lab)

    wait_recv(att, S_ATT)
    loads[2].wait()
    mid[...] = tokens[...].astype(F32) + dot(att[...], wtok[2])
    mid32 = mid[...]
    mlp_in[c] = (mid32 * scale_of(mid32) * mlp_gain[...]).astype(BF16)
    remote(mlp_in.at[c], mlp_in.at[c], S_MIN, partner).start()

    loads[3].wait()
    loads[4].wait()
    wait_recv(mlp_in.at[other], S_MIN)
    ring_end("uy")
    both = mlp_in[...].reshape(2 * rows, width)
    for n in range(nz // 2):
        piece = jnp.concatenate([up[2 * n], up[2 * n + 1]], axis=1)
        hid[:, n * 256 : (n + 1) * 256] = gelu(dot(both, piece)).astype(BF16)

    wait_recv(lab.at[pl.ds(0, ng - 1)], S_AG)
    attended = lab[...].reshape(ng * 32, PAIR)
    sq[...] = jnp.broadcast_to(jnp.sum(attended * attended, axis=0, keepdims=True), (8, PAIR))
    remote(sq, sq_in, S_SQ, partner).start()

    ring_end("dx")
    half_width = width // 2
    step = min(256, half_width)

    def mlp_out(first, last, slot):
        for n in range(first, last, step):
            span = slice(n, n + step)
            made = dot(hid[...], down[:, :, span].reshape(hid.shape[1], step))
            mp[:, :, span] = made.reshape(2, rows, step)
        span = pl.ds(first, last - first)
        remote(mp.at[other, :, span], mp_in.at[:, span], slot, partner).start()

    mlp_out(0, half_width, S_MP0)

    wait_recv(sq_in, S_SQ)
    norm = lax.rsqrt((sq[0:1, :] + sq_in[0:1, :]) * (1.0 / width) + NORM_EPS)
    mixed = (attended * norm).T.astype(BF16)
    wait_recv(wout, S_WOUT)
    part[...] = dot(mixed, wout[...]).reshape(2, 64, PAIR)
    remote(part.at[other], part_in, S_PART, partner).start()

    mlp_out(half_width, width, S_MP1)

    wait_recv(part_in, S_PART)
    own_lanes = lanes(gpair)
    latents_out[:, own_lanes] = (
        latents[:, own_lanes].astype(F32) + (part[c] + part_in[...])
    ).astype(BF16)

    def send_lo(k):
        device = (2 * lax.rem(gpair + k, nz) + lax.rem(g, 2), m)
        remote(latents_out.at[:, own_lanes], latents_out.at[:, own_lanes], S_LO, device).start()

    each(1, nz, send_lo)

    for first, slot in ((0, S_MP0), (half_width, S_MP1)):
        span = slice(first, first + half_width)
        wait_recv(mp_in.at[:, pl.ds(first, half_width)], slot)
        tokens_out[:, span] = (mid[:, span] + (mp[c, :, span] + mp_in[:, span])).astype(BF16)

    wait_recv(latents_out.at[:, pl.ds(0, (nz - 1) * PAIR)], S_LO)

    @pl.when(y != 0)
    def _():
        wait_send(latx.at[0, 0], S_LAT)

    for _ in range(2 * high - 1):
        wait_send(latx.at[0, 0], S_LAT)

    @pl.when(owner != z)
    def _():
        wait_send(zb, S_ZC)

    wait_send(lab.at[pl.ds(0, ng - 1)], S_AG)
    wait_send(wlat.at[pl.ds(0, nm - 1), 0], S_W)
    wait_send(wlat.at[:, pl.ds(0, nx - 1)], S_W2)
    wait_send(up.at[rest, up_piece, :], S_UP1)
    wait_send(down.at[rest, down_piece[0], down_piece[1]], S_DOWN1)
    wait_send(rv.at[0, rest], S_REF)
    wait_send(rv.at[1, rest], S_VAL)
    wait_send(wout.at[pl.ds(0, (nz - 1) * 64), :], S_WOUT)
    wait_send(others, S_PROJ)
    wait_send(lat_rv.at[0], S_PROJ2)
    for name in rings:
        ring_sent(name)
    wait_send(att_out.at[pl.ds(1, nz - 1)], S_ATT)
    wait_send(col_in, S_COL)
    wait_send(mlp_in.at[0], S_MIN)
    wait_send(rs.at[pl.ds(0, ng - 1)], S_RS)
    wait_send(sq_in, S_SQ)
    wait_send(part_in, S_PART)
    wait_send(mp_in.at[:, pl.ds(0, half_width)], S_MP0)
    wait_send(mp_in.at[:, pl.ds(half_width, half_width)], S_MP1)
    wait_send(latents_out.at[:, pl.ds(0, (nz - 1) * PAIR)], S_LO)


def per_device(nx, ny, nz, *args):
    (tokens, latents, tok_gain, lat_gain, mlp_gain, *weights) = args
    ng = nx * ny
    rows, width = tokens.shape
    lat_count = latents.shape[0] * 2 * nz
    unit = weights[6].shape[1]
    vmem = pl.BlockSpec(memory_space=pltpu.VMEM)
    anywhere = pl.BlockSpec(memory_space=pl.ANY)
    scratch = [
        ((3, width, width), BF16),
        ((nz, width, unit), BF16),
        ((nz, unit, width), BF16),
        ((2 * nz, nx, 64 // nx, PAIR), BF16),
        ((nz // ny, 2, 64 // nx, width), BF16),
        ((nz * 64, PAIR), BF16),
        ((2, nz, rows, PAIR), BF16),
        ((2, nz, rows, PAIR), BF16),
        ((2, nz // ny, ny, 2, nx, 64 // nx, PAIR), BF16),
        ((2, lat_count, PAIR), BF16),
        ((2, lat_count, PAIR), BF16),
        ((2, nz, rows, lat_count), F32),
        ((2, 8, lat_count), F32),
        ((2, 80, lat_count), F32),
        ((nz, rows, PAIR), BF16),
        ((rows, width), BF16),
        ((80, lat_count), F32),
        ((ng, 40, PAIR), F32),
        ((ng, 40, PAIR), F32),
        ((32, PAIR), F32),
        ((ng, 32, PAIR), F32),
        ((8, PAIR), F32),
        ((8, PAIR), F32),
        ((2, 64, PAIR), F32),
        ((64, PAIR), F32),
        ((rows, width), F32),
        ((2, rows, width), BF16),
        ((2 * rows, nz * unit), BF16),
        ((2, rows, width), F32),
        ((rows, width), F32),
    ]
    return pl.pallas_call(
        functools.partial(kernel, nx, ny, nz),
        out_shape=(
            jax.ShapeDtypeStruct(tokens.shape, BF16),
            jax.ShapeDtypeStruct(latents.shape, BF16),
        ),
        in_specs=[vmem] * 5 + [anywhere] * 8,
        out_specs=(vmem, vmem),
        scratch_shapes=[pltpu.VMEM(shape, kind) for shape, kind in scratch]
        + [
            pltpu.SemaphoreType.DMA((5,)),
            pltpu.SemaphoreType.DMA((S_REF + 1,)),
            pltpu.SemaphoreType.DMA((S_REF + nz,)),
            pltpu.SemaphoreType.REGULAR((2,)),
        ],
        compiler_params=pltpu.CompilerParams(
            collective_id=0, has_side_effects=True, vmem_limit_bytes=56 * 1024 * 1024
        ),
        name="layer",
    )(
        tokens,
        latents,
        tok_gain.reshape(1, width),
        lat_gain.reshape(1, width),
        mlp_gain.reshape(1, width),
        *weights,
    )


def solution(mesh):
    ng = mesh.shape["group"]
    nz = mesh.shape["member"] // 2
    nx = int(round(ng**0.5))
    in_specs = (
        P(("group", "member"), None),
        P("member", None),
        P(),
        P(),
        P(),
        P(),
        P(),
        P(),
        P("member", None),
        P("member", None),
        P("member", None),
        P(None, "member"),
        P("member", None),
    )
    out_specs = (P(("group", "member"), None), P("member", None))
    return jax.shard_map(
        functools.partial(per_device, nx, ng // nx, nz),
        mesh=mesh, in_specs=in_specs, out_specs=out_specs, check_vma=False,
    )
```
